256 devices in a mesh: pipe: 4 (over z_lo), dp: 2 (over z_hi), expert: 32 (over y, x, core).
Axes of the slice: x: 4, y: 4, z: 8 (z_hi: 2, z_lo: 4; z = z_hi * 4 + z_lo), core: 2. Of those that a mesh axis runs over, the one named last changes fastest.
Arguments:
- x_fwd: bfloat16 [4, 4096, 3584], P('pipe', ('dp', 'expert')), may hold values from -6 to 6
- routes_fwd: int32 [4, 4096, 2], P('pipe', ('dp', 'expert')), may hold values from 0 to 31, all different within a row; in each aligned block of 64 rows (0 to 63, 64 to 127, ..., all dimensions but the last counted through in order) at most 6 rows name the same one
- x_bwd: bfloat16 [4, 4096, 3584], P('pipe', ('dp', 'expert')), may hold values from -6 to 6
- cot_bwd: bfloat16 [4, 4096, 3584], P('pipe', ('dp', 'expert')), may hold values from -6 to 6
- routes_bwd: int32 [4, 4096, 2], P('pipe', ('dp', 'expert')), may hold values from 0 to 31, all different within a row; in each aligned block of 64 rows (0 to 63, 64 to 127, ..., all dimensions but the last counted through in order) at most 6 rows name the same one
- router_weight: bfloat16 [4, 3584, 32], P('pipe'), may hold values from -0.09375 to 0.09375
- gate_weight: bfloat16 [4, 32, 3584, 1024], P('pipe', 'expert', None, 'dp'), may hold values from -0.09375 to 0.09375
- up_weight: bfloat16 [4, 32, 3584, 1024], P('pipe', 'expert', None, 'dp'), may hold values from -0.09375 to 0.09375
- down_weight: bfloat16 [4, 32, 1024, 3584], P('pipe', 'expert', 'dp'), may hold values from -0.1875 to 0.1875
- attn_input: bfloat16 [4, 4096, 3584], P('pipe', ('dp', 'expert')), may hold values from -16 to 16
- latent_cot: bfloat16 [4, 4096, 512], P('pipe', ('dp', 'expert')), may hold values from -0.09375 to 0.09375
Outputs:
- fwd_sent: bfloat16 [4, 4096, 3584], P('pipe', ('dp', 'expert'))
- bwd_sent: bfloat16 [4, 4096, 3584], P('pipe', ('dp', 'expert'))
- kv_grad: float32 [4, 3584, 512], P('pipe', ('dp', 'expert'))
The draws below stay inside these ranges and needn't reach their ends.
Inputs may be any that keep to these rules, and one draw needn't show every extreme that they name: `routes_fwd`: A token names 2 different experts; in each block of 64 consecutive tokens of a section no expert is named by more than 6 routes, a bound that some block reaches. `routes_bwd`: A token names 2 different experts; in each block of 64 consecutive tokens of a section no expert is named by more than 6 routes, a bound that some block reaches.
All inputs are finite; a program needn't handle non-finite values.
Results may differ from the reference program's by a relative error of at most 0.0054.
Values may be sent and summed in bfloat16 or wider, within the bound.
A program may use at most 128 MiB of HBM per device.

```python
import math
from functools import partial
import jax
import jax.numpy as jnp
import numpy as np
from jax import lax

D = 3584
HID = 1024
LATENT = 512
TOP = 2
TOK_DEV = 64
SECTIONS = 4
EXPERTS = 32
CAP = 6
TOKENS = 4096
N_DP = 2
N_EXPERT = 32


def spiked(result, rng, source, target, shards_of, factor):
    def block_of(dim):
        return (jnp.arange(result.shape[dim]) // (result.shape[dim] // shards_of)).reshape((-1,) + (1,) * (result.ndim - 1 - dim))

    first = jax.random.permutation(rng, shards_of)[block_of(target)]
    second = (block_of(target) + shards_of // 2) % shards_of
    return jnp.where((block_of(source) == first) | (block_of(source) == second), factor * result, result)


def levels(rng, shape, shards, smallest, high):
    def one(dim, parts):
        heights = jax.random.uniform(jax.random.fold_in(jax.random.fold_in(rng, 6), dim), (parts,), jnp.float32, smallest / len(shards), high / len(shards))
        return jnp.repeat(jnp.exp(heights), shape[dim] // parts).reshape((-1,) + (1,) * (len(shape) - dim - 1))

    factor_of = one(*shards[0])
    for cut in shards[1:]:
        factor_of = factor_of * one(*cut)
    return factor_of


def assign_block(key, own, number, rows, count, top, bound, lean):
    sequence = jax.random.permutation(key, count)
    heavy_load, common = portions_of(count, rows * top, bound, lean, True), portions_of(count, rows * top, bound, lean, False)
    places = jnp.arange(count)

    def named(sizes, turn):
        used = int((sizes > 0).sum())
        fixed = max(1, used // 4)
        shifted = fixed + (places - fixed + turn * (used - fixed)) % max(1, count - fixed)
        return jnp.zeros((count,), jnp.int32).at[sequence[jnp.where(places < fixed, places, shifted)]].set(jnp.asarray(sizes, jnp.int32))

    sizes = jnp.where(number % 4 == 0, named(heavy_load, number // 4), named(common, number - number // 4 - 1))
    mixed = jax.random.permutation(jax.random.fold_in(own, 3), count)
    source_of, taker = mixed[0:count // 2 * 2:2], mixed[1:count // 2 * 2:2]
    margin = jnp.minimum(sizes[source_of] - 1, bound - sizes[taker]) // 2
    margin = jnp.where((source_of == sequence[0]) | (taker == sequence[0]) | (sizes[taker] == 0), 0, jnp.maximum(margin, 0))
    shifted = jax.random.randint(jax.random.fold_in(own, 4), (count // 2,), 0, 1 << 20) % (margin + 1)
    sizes = sizes.at[source_of].add(-shifted).at[taker].add(shifted)
    labels = jnp.searchsorted(jnp.cumsum(sizes), jnp.arange(rows * top), side="right").astype(jnp.int32)
    table = labels.reshape(top, rows).T
    table = table[jax.random.permutation(jax.random.fold_in(own, 1), rows)]
    turn = jax.random.randint(jax.random.fold_in(own, 2), (rows, 1), 0, top)
    return jnp.take_along_axis(table, (jnp.arange(top)[None, :] + turn) % top, axis=1)


def portions_of(amount, total, reach, lean, full):
    weights = [(1 << 20) // math.isqrt(rank ** lean) + 1 for rank in range(1, amount + 1)]
    largest = reach if full else min(reach, max(-(-total // amount), total * weights[0] // sum(weights)))
    least = 1 if total - largest >= amount - 1 else 0
    counts, spare = [largest] + [least] * (amount - 1), total - largest - least * (amount - 1)
    while spare > 0:
        movable = [i for i in range(1, amount) if counts[i] < largest] or [i for i in range(1, amount) if counts[i] < reach]
        mass, left = sum([weights[i] for i in movable]), spare
        for i in movable:
            more = min(reach - counts[i], max(1, left * weights[i] // mass), spare)
            counts[i] = counts[i] + more
            spare = spare - more
    return np.array(counts)


def noise(rng, dims, deviation, bound, split=(), kind=jnp.bfloat16):
    gain = levels(rng, dims, split, -0.22, 0.18) if split else 1.0
    values = jax.random.normal(rng, dims, jnp.float32) * deviation * gain
    return jnp.minimum(jnp.maximum(values, -bound), bound).astype(kind)


def gaussian_with(own_key, shape, width, most, shards, heavy, held_as=jnp.bfloat16):
    result = width * jax.random.normal(own_key, shape, jnp.float32)
    if shards:
        result = result * levels(own_key, shape, shards, -0.22, 0.18)
    return jnp.clip(spiked(result, jax.random.fold_in(own_key, 3), *heavy), -most, most).astype(held_as)


def setup_inputs(seed: int = 0) -> dict:
    key_of = jax.random.split(jax.random.key(seed), 12)
    x_fwd = noise(key_of[0], (SECTIONS, TOKENS, D), 1.0, 6.0, ((0, 4), (1, 64)))
    routes_fwd_keys = jax.random.split(jax.random.fold_in(key_of[1], 1), SECTIONS * TOKENS // TOK_DEV)
    routes_fwd_turns = jax.random.permutation(jax.random.fold_in(key_of[1], 3), SECTIONS * TOKENS // TOK_DEV)
    routes_fwd = jax.vmap(lambda own, number: assign_block(jax.random.fold_in(key_of[1], 2), own, number, TOK_DEV, EXPERTS, TOP, CAP, 1))(routes_fwd_keys, routes_fwd_turns).reshape((SECTIONS, TOKENS, TOP))
    x_bwd = noise(key_of[2], (SECTIONS, TOKENS, D), 1.0, 6.0, ((0, 4), (1, 64)))
    cot_bwd = noise(key_of[3], (SECTIONS, TOKENS, D), 1.0, 6.0, ((0, 4), (1, 64)))
    routes_bwd_keys = jax.random.split(jax.random.fold_in(key_of[4], 1), SECTIONS * TOKENS // TOK_DEV)
    routes_bwd_turns = jax.random.permutation(jax.random.fold_in(key_of[4], 3), SECTIONS * TOKENS // TOK_DEV)
    routes_bwd = jax.vmap(lambda own, number: assign_block(jax.random.fold_in(key_of[4], 2), own, number, TOK_DEV, EXPERTS, TOP, CAP, 1))(routes_bwd_keys, routes_bwd_turns).reshape((SECTIONS, TOKENS, TOP))
    router_weight = noise(key_of[5], (SECTIONS, D, EXPERTS), D ** -0.5, 0.09375, ((0, 4),))
    gate_weight = noise(key_of[6], (SECTIONS, EXPERTS, D, HID), D ** -0.5, 0.09375, ((0, 4), (1, 32), (3, 2)))
    up_weight = noise(key_of[7], (SECTIONS, EXPERTS, D, HID), D ** -0.5, 0.09375, ((0, 4), (1, 32), (3, 2)))
    down_weight = noise(key_of[8], (SECTIONS, EXPERTS, HID, D), HID ** -0.5, 0.1875, ((0, 4), (1, 32), (2, 2)))
    attn_input = gaussian_with(key_of[9], (SECTIONS, TOKENS, D), 1.0, 16.0, ((0, 4), (1, 64)), (1, 2, 64, 4.0))
    latent_cot = noise(key_of[10], (SECTIONS, TOKENS, LATENT), (TOKENS ** -0.5), 0.09375, ((0, 4), (1, 64)))
    return {"x_fwd": x_fwd, "routes_fwd": routes_fwd, "x_bwd": x_bwd, "cot_bwd": cot_bwd, "routes_bwd": routes_bwd, "router_weight": router_weight, "gate_weight": gate_weight, "up_weight": up_weight, "down_weight": down_weight, "attn_input": attn_input, "latent_cot": latent_cot}


ROUTE_SCALE = 2.5

def slot_keys(routes, count_experts, capacity):
    route_count = routes.shape[0] * routes.shape[1]
    flat_routes = routes.reshape(route_count)
    expert_ids = jnp.arange(count_experts, dtype=jnp.int32)
    member = (flat_routes[:, None] == expert_ids[None, :]).astype(jnp.int32)
    earlier = jnp.cumsum(member, axis=0) - member
    slot_index = lax.optimization_barrier(jnp.sum(earlier * member, axis=1))
    return (flat_routes * capacity + slot_index).reshape(routes.shape).astype(jnp.int32)

def place_rows(slot_key, tokens, positions):
    targets = jnp.arange(positions, dtype=jnp.int32)
    member = lax.optimization_barrier(jnp.sum((slot_key[None, :, :] == targets[:, None, None]).astype(jnp.float32), axis=2))
    placed = jnp.dot(member.astype(jnp.bfloat16), tokens, preferred_element_type=jnp.float32)
    return placed.astype(jnp.bfloat16)

def route_gates(tokens, router, routes):
    logits = jnp.dot(tokens, router, preferred_element_type=jnp.float32)
    expert_ids = jnp.arange(router.shape[1], dtype=jnp.int32)
    route_table = (routes[:, :, None] == expert_ids[None, None, :]).astype(jnp.float32)
    chosen = lax.optimization_barrier(jnp.sum(logits[:, None, :] * route_table, axis=2))
    route_rates = jax.nn.sigmoid(chosen)
    rate_total = lax.optimization_barrier(jnp.sum(route_rates, axis=1, keepdims=True))
    return (ROUTE_SCALE * route_rates / rate_total, route_rates, rate_total, route_table)

def expert_forward(row_block, gate_matrix, up_matrix, down_matrix):
    gate_act = jnp.dot(row_block, gate_matrix, preferred_element_type=jnp.float32)
    up_act = jnp.dot(row_block, up_matrix, preferred_element_type=jnp.float32)
    hidden = (gate_act * jax.nn.sigmoid(gate_act) * up_act).astype(jnp.bfloat16)
    return jnp.dot(hidden, down_matrix, preferred_element_type=jnp.float32)

def expert_backward(row_block, cotangent, gate_matrix, up_matrix, down_matrix):
    gate_act = jnp.dot(row_block, gate_matrix, preferred_element_type=jnp.float32)
    up_act = jnp.dot(row_block, up_matrix, preferred_element_type=jnp.float32)
    sigmoid_gate = jax.nn.sigmoid(gate_act)
    active = gate_act * sigmoid_gate
    hidden = (active * up_act).astype(jnp.bfloat16)
    full_out = jnp.dot(hidden, down_matrix, preferred_element_type=jnp.float32)
    inner_dot = lax.optimization_barrier(jnp.sum(cotangent.astype(jnp.float32) * full_out, axis=1))
    contract = (((1,), (1,)), ((), ()))
    grad_hidden = lax.dot_general(cotangent, down_matrix, contract, preferred_element_type=jnp.float32)
    grad_gate = (grad_hidden * up_act * sigmoid_gate * (1.0 + gate_act * (1.0 - sigmoid_gate))).astype(jnp.bfloat16)
    grad_up = (grad_hidden * active).astype(jnp.bfloat16)
    back_rows = lax.dot_general(grad_gate, gate_matrix, contract, preferred_element_type=jnp.float32)
    back_rows = back_rows + lax.dot_general(grad_up, up_matrix, contract, preferred_element_type=jnp.float32)
    return (back_rows, inner_dot)

def combine_rows(gates, slot_key, returned):
    picked = jnp.take(returned, slot_key.reshape(-1), axis=0)
    picked = picked.reshape(slot_key.shape + (returned.shape[1],))
    return lax.optimization_barrier(jnp.sum(gates[:, :, None] * picked.astype(jnp.float32), axis=1))

def router_grad(route_rates, rate_total, route_table, inner_picked):
    weighted = lax.optimization_barrier(jnp.sum(inner_picked * route_rates, axis=1, keepdims=True))
    grad_rates = ROUTE_SCALE * (inner_picked / rate_total - weighted / (rate_total * rate_total))
    grad_logit = grad_rates * route_rates * (1.0 - route_rates)
    return lax.optimization_barrier(jnp.sum(grad_logit[:, :, None] * route_table, axis=1)).astype(jnp.bfloat16)

def source_side(router, tok_fwd, key_fwd, route_fwd, ret_fwd, tok_bwd, cotangent, key_bwd, route_bwd, ret_back, ret_inner):
    gates_fwd = route_gates(tok_fwd, router, route_fwd)[0]
    y_fwd = (tok_fwd.astype(jnp.float32) + combine_rows(gates_fwd, key_fwd, ret_fwd)).astype(jnp.bfloat16)
    gates_bwd, route_rates, rate_total, route_table = route_gates(tok_bwd, router, route_bwd)
    inner_picked = jnp.take(ret_inner, key_bwd.reshape(-1), axis=0).reshape(key_bwd.shape).astype(jnp.float32)
    grad_logits = router_grad(route_rates, rate_total, route_table, inner_picked)
    router_back = lax.dot_general(grad_logits, router, (((1,), (1,)), ((), ())), preferred_element_type=jnp.float32)
    dx_bwd = cotangent.astype(jnp.float32) + combine_rows(gates_bwd, key_bwd, ret_back) + router_back
    return (y_fwd, dx_bwd.astype(jnp.bfloat16))

def section_pass(x_fwd, routes_fwd, x_bwd, cot_bwd, routes_bwd, router, gate_all, up_all, down_all):
    blocks = N_DP * N_EXPERT
    positions = EXPERTS * CAP

    def split_blocks(array):
        return array.reshape((blocks, TOK_DEV) + array.shape[1:])
    keys_fwd = jax.vmap(partial(slot_keys, count_experts=EXPERTS, capacity=CAP))(split_blocks(routes_fwd))
    keys_bwd = jax.vmap(partial(slot_keys, count_experts=EXPERTS, capacity=CAP))(split_blocks(routes_bwd))

    def dispatch(slot_key, tokens):
        placed = jax.vmap(partial(place_rows, positions=positions))(slot_key, tokens)
        placed = placed.reshape(blocks, EXPERTS, CAP, D).transpose(1, 0, 2, 3)
        return placed.reshape(EXPERTS, blocks * CAP, D)
    disp_fwd = dispatch(keys_fwd, split_blocks(x_fwd))
    disp_x = dispatch(keys_bwd, split_blocks(x_bwd))
    disp_g = dispatch(keys_bwd, split_blocks(cot_bwd))

    def per_expert(expert_items):
        rows_fwd, rows_x, rows_g, gate_matrix, up_matrix, down_matrix = expert_items
        out_fwd = expert_forward(rows_fwd, gate_matrix, up_matrix, down_matrix).astype(jnp.bfloat16)
        back_rows, inner_dot = expert_backward(rows_x, rows_g, gate_matrix, up_matrix, down_matrix)
        return (out_fwd, back_rows.astype(jnp.bfloat16), inner_dot.astype(jnp.bfloat16))
    out_fwd, out_back, out_inner = lax.map(per_expert, (disp_fwd, disp_x, disp_g, gate_all, up_all, down_all))

    def undo(array):
        shaped = array.reshape((EXPERTS, blocks, CAP) + array.shape[2:])
        order = (1, 0, 2) + tuple(range(3, shaped.ndim))
        return shaped.transpose(order).reshape((blocks, positions) + array.shape[2:])
    y_fwd, dx_bwd = jax.vmap(partial(source_side, router))(split_blocks(x_fwd), keys_fwd, split_blocks(routes_fwd), undo(out_fwd), split_blocks(x_bwd), split_blocks(cot_bwd), keys_bwd, split_blocks(routes_bwd), undo(out_back), undo(out_inner))
    return (y_fwd.reshape(TOKENS, D), dx_bwd.reshape(TOKENS, D))

def reference(x_fwd, routes_fwd, x_bwd, cot_bwd, routes_bwd, router_weight, gate_weight, up_weight, down_weight, attn_input, latent_cot):
    forward_list = []
    backward_list = []
    kv_list = []
    for section_index in range(SECTIONS):
        y_fwd, dx_bwd = section_pass(x_fwd[section_index], routes_fwd[section_index], x_bwd[section_index], cot_bwd[section_index], routes_bwd[section_index], router_weight[section_index], gate_weight[section_index], up_weight[section_index], down_weight[section_index])
        forward_list.append(y_fwd)
        backward_list.append(dx_bwd)
        kv_list.append(lax.dot_general(attn_input[section_index], latent_cot[section_index], (((0,), (0,)), ((), ())), preferred_element_type=jnp.float32))
    fwd_sent = jnp.roll(jnp.stack(forward_list), 1, axis=0)
    bwd_sent = jnp.roll(jnp.stack(backward_list), 1, axis=0)
    return (fwd_sent, bwd_sent, jnp.stack(kv_list))
```

```python
import functools

import jax
import jax.numpy as jnp
import numpy as np
from jax import lax
from jax.experimental import pallas as pl
from jax.experimental.pallas import tpu as pltpu
from jax.sharding import PartitionSpec as P

TOP = 2
ROUTE_SCALE = 2.5
CAP = 6
TOK = 64
D = 3584
EXPERTS = 32
HALF = 512
LATENT = 512
Q = 4
PIECE = D // Q
S = 7
PART = D // S
SLOT = 2 * CAP * Q
WIRE = EXPERTS * SLOT
ROWS = EXPERTS * CAP
CHUNK = 8
KV_ROWS = 56
MESH = pl.DeviceIdType.MESH
BF = jnp.bfloat16
F32 = jnp.float32

STEPS = [(2, 2), (1, 0), (3, 0), (0, 1), (0, 3), (2, 0), (0, 2), (1, 1), (3, 3), (1, 3), (3, 1), (2, 1), (1, 2), (2, 3), (3, 2)]
STEPS_X = sum(x * 4**i for i, (x, _) in enumerate(STEPS))
STEPS_Y = sum(y * 4**i for i, (_, y) in enumerate(STEPS))


def permutations():
    unpack = np.zeros((CHUNK * SLOT, CHUNK * SLOT), np.float32)
    pack_part = np.zeros((CHUNK * SLOT, S * CHUNK * CAP), np.float32)
    pack_inner = np.zeros((EXPERTS * 16, 2 * ROWS), np.float32)
    for s in range(CHUNK):
        for slot in range(CAP):
            for q in range(Q):
                for j in range(2):
                    unpack[j * 192 + q * 48 + s * CAP + slot, s * SLOT + q * 12 + j * CAP + slot] = 1
            for q in range(S):
                pack_part[s * SLOT + q * CAP + slot, q * 48 + s * CAP + slot] = 1
    for s in range(EXPERTS):
        for j in range(2):
            for slot in range(CAP):
                pack_inner[s * 16 + j * CAP + slot, j * ROWS + s * CAP + slot] = 1
    return unpack, unpack.T.copy(), pack_part, pack_inner


def dot(a, b):
    return jnp.dot(a, b, preferred_element_type=F32)


def dot_nt(a, b):
    return lax.dot_general(a, b, (((1,), (1,)), ((), ())), preferred_element_type=F32)


def kernel(
    xf, xb, cg, meta, router, unpack, pack, pack_part, pack_inner,
    gate_hbm, up_hbm, down_hbm, attn_hbm, latent_hbm,
    fwd_out, bwd_out, kv_out,
    gate, up, down, stack_f, stack_own, stack_peer, meta_peer,
    w1, w2, w3, a1, a2, a3, x2, gg, gu, hid, inner,
    fo_own, fo_peer, fo_got, back, a4, a5, part,
    iv_wire, iv_got, g_fwd, g_bwd, acc, peer_part, peer_got, val, val_send, val_got,
    attn_got, latent_got, kv_sum, kv_got, y_send, dx_send, y_got, dx_got,
    load_sem, z_send, z_recv, u_send, u_recv, local_sem, p_send, p_recv,
):
    pi, dp, ex = lax.axis_index("pipe"), lax.axis_index("dp"), lax.axis_index("expert")
    core = lax.rem(ex, 2)
    px = lax.rem(lax.div(ex, 2), 4)
    py = lax.div(ex, 8)
    zpeer = (pi, 1 - dp, ex)
    ahead = (lax.rem(pi + 1, 4), dp, ex)
    behind = (lax.rem(pi + 3, 4), dp, ex)

    loads = [
        pltpu.make_async_copy(src, dst, load_sem.at[i])
        for i, (src, dst) in enumerate([(gate_hbm, gate), (up_hbm, up), (down_hbm, down)])
    ]

    barrier = pltpu.get_barrier_semaphore()
    pl.semaphore_signal(barrier, inc=1, device_id=zpeer, device_id_type=MESH)
    pl.semaphore_signal(barrier, inc=1, device_id=ahead, device_id_type=MESH)
    pl.semaphore_signal(barrier, inc=1, device_id=behind, device_id_type=MESH)

    def greet(o, c):
        pl.semaphore_signal(barrier, inc=1, device_id=(pi, dp, lax.rem(ex + o, EXPERTS)), device_id_type=MESH)
        return c

    lax.fori_loop(1, EXPERTS, greet, 0)
    for load in loads:
        load.start()

    def plane(unit, src, dst, rows, one_source=False, cols=None):
        def piece(e):
            at = pl.ds(pl.multiple_of(e * rows, 16), rows)
            if one_source:
                return src
            return src.at[at] if cols is None else src.at[at, pl.ds(0, cols)]

        def copy(i, dx, dy, dc):
            to = (lax.rem(py + dy, 4) * 4 + lax.rem(px + dx, 4)) * 2 + lax.rem(core + dc, 2)
            return pltpu.make_async_remote_copy(
                src_ref=piece(to),
                dst_ref=dst.at[pl.ds(pl.multiple_of(ex * rows, 16), rows)],
                send_sem=u_send.at[unit, i],
                recv_sem=u_recv.at[unit, i],
                device_id=(pi, dp, to),
                device_id_type=MESH,
            )

        def local():
            return pltpu.make_async_copy(
                piece(ex),
                dst.at[pl.ds(pl.multiple_of(ex * rows, 16), rows)],
                local_sem.at[unit],
            )

        def start():
            def step(i, c):
                tx, ty = c
                dx, dy = lax.rem(tx, 4), lax.rem(ty, 4)
                copy(2 * i, dx, dy, 0).start()
                copy(2 * i + 1, dx, dy, 1).start()
                return lax.div(tx, 4), lax.div(ty, 4)

            lax.fori_loop(0, 15, step, (jnp.int32(STEPS_X), jnp.int32(STEPS_Y)))
            copy(30, 0, 0, 1).start()
            local().start()

        def wait_recv():
            def step(i, c):
                pltpu.make_async_copy(dst.at[pl.ds(0, rows)], dst.at[pl.ds(0, rows)], u_recv.at[unit, i]).wait()
                return c

            lax.fori_loop(0, 31, step, 0)
            local().wait()

        def wait_send():
            def step(i, c):
                pltpu.make_async_copy(dst.at[pl.ds(0, rows)], dst.at[pl.ds(0, rows)], u_send.at[unit, i]).wait()
                return c

            lax.fori_loop(0, 31, step, 0)

        return start, wait_recv, wait_send

    def to_zpeer(i, src, dst):
        return pltpu.make_async_remote_copy(
            src_ref=src, dst_ref=dst, send_sem=z_send.at[i], recv_sem=z_recv.at[i], device_id=zpeer, device_id_type=MESH
        )

    def place(code_a, code_b, stack, wire):
        first = jnp.concatenate([code_a[0:1], code_b[0:1] + float(CAP)], axis=1).astype(jnp.int32)
        second = jnp.concatenate([code_a[1:2], code_b[1:2] + float(CAP)], axis=1).astype(jnp.int32)

        def step(g, c):
            row = lax.broadcasted_iota(jnp.int32, (192, 512), 0) + g * 192
            member = jnp.where((row == first) | (row == second), 1.0, 0.0).astype(BF)
            wire[pl.ds(pl.multiple_of(g * 192, 16), 192), :] = dot(member, stack[...]).astype(BF)
            return c

        lax.fori_loop(0, 8, step, 0)

    def unpacked(wire):
        def step(c, carry):
            rows = dot(unpack[...], wire[pl.ds(pl.multiple_of(c * 384, 16), 384), :]).astype(BF)
            for j in range(2):
                for q in range(Q):
                    x2[pl.ds(pl.multiple_of(j * ROWS + c * 48, 16), 48), q * PIECE : (q + 1) * PIECE] = rows[
                        j * 192 + q * 48 : j * 192 + (q + 1) * 48
                    ]
            return carry

        lax.fori_loop(0, 4, step, 0)

    for q in range(Q):
        cols = slice(q * PIECE, (q + 1) * PIECE)
        stack_f[q * TOK : (q + 1) * TOK, :] = xf[:, cols]
        stack_own[q * TOK : (q + 1) * TOK, :] = xb[:, cols]
        stack_own[256 + q * TOK : 256 + (q + 1) * TOK, :] = cg[:, cols]
    own = meta[...]
    place(own[2:4], own[2:4], stack_own, w1)

    pl.semaphore_wait(barrier, 34)
    z_meta = to_zpeer(0, meta, meta_peer)
    z_f = to_zpeer(1, stack_f.at[pl.ds(0, 256)], stack_f.at[pl.ds(256, 256)])
    z_xg = to_zpeer(2, stack_own, stack_peer)
    z_meta.start()
    z_f.start()
    start1, recv1, sent1 = plane(0, w1, a1, SLOT)
    start1()
    z_meta.wait_recv()
    peer = meta_peer[...]
    z_f.wait_recv()
    z_xg.start()
    place(own[0:2], peer[0:2], stack_f, w2)
    start2, recv2, sent2 = plane(1, w2, a2, SLOT)
    start2()

    own_t, peer_t = own.T, peer.T

    def split(values):
        hi = values.astype(BF)
        return hi, (values - hi.astype(F32)).astype(BF)

    lane = lax.broadcasted_iota(jnp.int32, (TOK, WIRE), 1)

    def gate_rows(code0, code1, gate0, gate1, offset):
        value = jnp.where(lane == code0.astype(jnp.int32) + offset, gate0, 0.0)
        value = value + jnp.where(lane == code1.astype(jnp.int32) + offset, gate1, 0.0)
        return split(value)

    for j, m in enumerate((own_t, peer_t)):
        for q in range(Q):
            m_q = m[q * TOK : (q + 1) * TOK]
            hi, lo = gate_rows(m_q[:, 2:3], m_q[:, 3:4], m_q[:, 4:5], m_q[:, 5:6], j * CAP)
            g_bwd[j * 512 + q * TOK : j * 512 + (q + 1) * TOK, :] = hi
            g_bwd[j * 512 + 256 + q * TOK : j * 512 + 256 + (q + 1) * TOK, :] = lo
    for q in range(S):
        m = own_t[0:TOK]
        hi, lo = gate_rows(m[:, 0:1], m[:, 1:2], m[:, 8:9], m[:, 9:10], q * CAP)
        g_fwd[q * TOK : (q + 1) * TOK, :] = hi
        g_fwd[S * TOK + q * TOK : S * TOK + (q + 1) * TOK, :] = lo

    def backward(j):
        total = jnp.zeros((ROWS, 1), F32)
        for n in range(HALF // 256):
            cols = slice(n * 256, (n + 1) * 256)
            gate_act = dot(x2[0:ROWS, :], gate[:, cols])
            up_act = dot(x2[0:ROWS, :], up[:, cols])
            grad_hidden = dot_nt(x2[ROWS : 2 * ROWS, :], down[cols, :])
            sig = jax.nn.sigmoid(gate_act)
            active = gate_act * sig
            hidden = (active * up_act).astype(BF).astype(F32)
            total = total + jnp.sum(hidden * grad_hidden, axis=1, keepdims=True)
            gg[:, cols] = (grad_hidden * up_act * sig * (1.0 + gate_act * (1.0 - sig))).astype(BF)
            gu[:, cols] = (grad_hidden * active).astype(BF)
        hi, lo = split(total)
        side = lax.broadcasted_iota(jnp.int32, (ROWS, 128), 1) < 64
        inner[j * ROWS : (j + 1) * ROWS, :] = jnp.where(side, hi.astype(F32), lo.astype(F32)).astype(BF)

        def step(q, c):
            cols = pl.ds(pl.multiple_of(q * PIECE, 128), PIECE)
            rows = (dot_nt(gg[...], gate[cols, :]) + dot_nt(gu[...], up[cols, :])).astype(BF)
            for g in range(4):
                back[pl.ds(pl.multiple_of(g * 384 + j * 192 + q * 48, 16), 48), :] = rows[g * 48 : (g + 1) * 48]
            return c

        lax.fori_loop(0, Q, step, 0)

    z_xg.wait_recv()
    place(peer[2:4], peer[2:4], stack_peer, w3)
    start3, recv3, sent3 = plane(2, w3, a3, SLOT)
    start3()

    for load in loads:
        load.wait()
    recv1()
    unpacked(a1)
    backward(0)

    recv2()
    unpacked(a2)
    for n in range(HALF // 256):
        cols = slice(n * 256, (n + 1) * 256)
        gate_act = dot(x2[...], gate[:, cols])
        up_act = dot(x2[...], up[:, cols])
        hid[:, cols] = (gate_act * jax.nn.sigmoid(gate_act) * up_act).astype(BF)

    def forward(q, c):
        cols = pl.ds(pl.multiple_of(q * PIECE, 128), PIECE)
        rows = dot(hid[...], down[:, cols]).astype(BF)
        fo_own[:, cols] = rows[0:ROWS]
        fo_peer[:, cols] = rows[ROWS : 2 * ROWS]
        return c

    lax.fori_loop(0, Q, forward, 0)
    z_out = to_zpeer(3, fo_peer, fo_got)
    z_out.start()

    recv3()
    unpacked(a3)
    backward(1)
    sent1()

    def pack_back(g, c):
        rows = pl.ds(pl.multiple_of(g * 384, 16), 384)
        w1[rows, :] = dot(pack[...], back[rows, :]).astype(BF)
        return c

    lax.fori_loop(0, 4, pack_back, 0)
    iv_wire[...] = dot(pack_inner[...], inner[...]).astype(BF)
    start4, recv4, sent4 = plane(3, w1, a4, SLOT)
    start_i, recv_i, sent_i = plane(4, iv_wire, iv_got, 16)
    start_i()
    start4()

    z_out.wait_recv()
    sent2()

    def pack_forward(g, c):
        rows = pl.ds(pl.multiple_of(g * 48, 16), 48)
        for q in range(S):
            cols = slice(q * PART, (q + 1) * PART)
            part[q * 48 : (q + 1) * 48, :] = (fo_own[rows, cols].astype(F32) + fo_got[rows, cols].astype(F32)).astype(BF)
        w2[pl.ds(pl.multiple_of(g * 384, 16), 384), 0:PART] = dot(pack_part[...], part[...]).astype(BF)
        return c

    lax.fori_loop(0, 4, pack_forward, 0)
    start5, recv5, sent5 = plane(5, w2, a5, SLOT, cols=PART)
    start5()
    start_a, recv_a, sent_a = plane(6, attn_hbm, attn_got, TOK)
    start_l, recv_l, sent_l = plane(7, latent_hbm, latent_got, TOK, one_source=True)
    start_a()
    start_l()

    recv_i()
    lane_i = lax.broadcasted_iota(jnp.int32, (TOK, EXPERTS * 16), 1)
    picks = []
    for j, m in enumerate((own_t, peer_t)):
        for k in range(TOP):
            code = m[0:TOK, 6 + k : 7 + k].astype(jnp.int32) + j * CAP
            picks.append(jnp.where(lane_i == code, 1.0, 0.0).astype(BF))
    val[...] = dot(jnp.concatenate(picks, axis=0), iv_got[...])
    val_send[...] = val[128:256, :].astype(BF)
    recv4()
    got = dot(g_bwd[512:1024, :], a4[...])
    peer_part[...] = (got[0:256] + got[256:512]).astype(BF)
    z_val = to_zpeer(4, val_send, val_got)
    z_part = to_zpeer(5, peer_part, peer_got)
    z_val.start()
    z_part.start()
    got = dot(g_bwd[0:512, :], a4[...])
    acc[...] = got[0:256] + got[256:512]

    def to_next(i, src, dst):
        return pltpu.make_async_remote_copy(
            src_ref=src, dst_ref=dst, send_sem=p_send.at[i], recv_sem=p_recv.at[i], device_id=ahead, device_id_type=MESH
        )

    recv5()
    got = dot(g_fwd[...], a5[...])
    for q in range(S):
        cols = slice(q * PART, (q + 1) * PART)
        y = xf[:, cols].astype(F32) + got[q * TOK : (q + 1) * TOK] + got[(S + q) * TOK : (S + q + 1) * TOK]
        y_send[:, cols] = y.astype(BF)
    n_y = to_next(0, y_send, y_got)
    n_y.start()

    z_val.wait_recv()
    inner0 = val[0:64, 0:1] + val[0:64, 64:65] + val_got[0:64, 0:1].astype(F32) + val_got[0:64, 64:65].astype(F32)
    inner1 = val[64:128, 0:1] + val[64:128, 64:65] + val_got[64:128, 0:1].astype(F32) + val_got[64:128, 64:65].astype(F32)
    m = own_t[0:TOK]
    rate0, rate1, rate_total = m[:, 10:11], m[:, 11:12], m[:, 12:13]
    weighted = (inner0 * rate0 + inner1 * rate1) / (rate_total * rate_total)
    logit0 = ROUTE_SCALE * (inner0 / rate_total - weighted) * rate0 * (1.0 - rate0)
    logit1 = ROUTE_SCALE * (inner1 / rate_total - weighted) * rate1 * (1.0 - rate1)
    lane_e = lax.broadcasted_iota(jnp.int32, (TOK, EXPERTS), 1)
    dlogits = jnp.where(lane_e == m[:, 13:14].astype(jnp.int32), logit0, 0.0)
    dlogits = (dlogits + jnp.where(lane_e == m[:, 14:15].astype(jnp.int32), logit1, 0.0)).astype(BF)
    for q in range(Q):
        cols = slice(q * PIECE, (q + 1) * PIECE)
        rows = slice(q * TOK, (q + 1) * TOK)
        acc[rows, :] = acc[rows, :] + dot_nt(dlogits, router[cols, :]) + cg[:, cols].astype(F32)
    z_part.wait_recv()
    for q in range(Q):
        rows = slice(q * TOK, (q + 1) * TOK)
        dx_send[:, q * PIECE : (q + 1) * PIECE] = (acc[rows, :] + peer_got[rows, :].astype(F32)).astype(BF)
    n_dx = to_next(1, dx_send, dx_got)
    n_dx.start()

    recv_a()
    recv_l()
    kv_sum[...] = lax.dot_general(attn_got[...], latent_got[...], (((0,), (0,)), ((), ())), preferred_element_type=F32)
    z_kv = to_zpeer(6, kv_sum.at[pl.ds(pl.multiple_of((1 - dp) * 64, 8), KV_ROWS)], kv_got)
    z_kv.start()
    z_kv.wait_recv()
    kv_out[...] = kv_sum[pl.ds(pl.multiple_of(dp * 64, 8), KV_ROWS), :] + kv_got[...]

    n_y.wait_recv()
    fwd_out[...] = y_got[...]
    n_dx.wait_recv()
    bwd_out[...] = dx_got[...]

    for sent in (sent3, sent4, sent_i, sent5, sent_a, sent_l):
        sent()
    for copy in (z_meta, z_f, z_xg, z_out, z_val, z_part, z_kv, n_y, n_dx):
        copy.wait_send()


def slot_keys(routes):
    flat = routes.reshape(TOK * TOP)
    member = (flat[:, None] == jnp.arange(EXPERTS, dtype=jnp.int32)[None, :]).astype(jnp.int32)
    earlier = jnp.cumsum(member, axis=0) - member
    return jnp.sum(earlier * member, axis=1).reshape(routes.shape)


def route_gates(tokens, router, routes):
    logits = jnp.dot(tokens, router, preferred_element_type=F32)
    table = (routes[:, :, None] == jnp.arange(EXPERTS, dtype=jnp.int32)[None, None, :]).astype(F32)
    rates = jax.nn.sigmoid(jnp.sum(logits[:, None, :] * table, axis=2))
    total = jnp.sum(rates, axis=1, keepdims=True)
    return ROUTE_SCALE * rates / total, rates, total


def body(x_fwd, routes_fwd, x_bwd, cot_bwd, routes_bwd, router_weight, gate_weight, up_weight, down_weight, attn_input, latent_cot):
    router = router_weight[0]
    rf, rb = routes_fwd[0], routes_bwd[0]
    slot_f, slot_b = slot_keys(rf), slot_keys(rb)
    gates_f, _, _ = route_gates(x_fwd[0], router, rf)
    gates_b, rates_b, total_b = route_gates(x_bwd[0], router, rb)
    offsets = jnp.repeat(jnp.arange(Q, dtype=F32) * 12, TOK)[None, :]

    def rows(values):
        return jnp.tile(values.astype(F32).T, (1, Q))

    meta = jnp.concatenate(
        [
            rows(rf * SLOT + slot_f) + offsets,
            rows(rb * SLOT + slot_b) + offsets,
            rows(gates_b),
            rows(rb * 16 + slot_b),
            rows(gates_f),
            rows(rates_b),
            rows(total_b),
            rows(rb),
            jnp.zeros((1, Q * TOK), F32),
        ],
        axis=0,
    )
    attn = attn_input[0].reshape(TOK, 2, EXPERTS, KV_ROWS).transpose(2, 0, 1, 3)
    attn = jnp.pad(attn, ((0, 0), (0, 0), (0, 0), (0, 64 - KV_ROWS))).reshape(EXPERTS * TOK, 128)
    consts = [jnp.asarray(c, BF) for c in permutations()]
    vmem = pl.BlockSpec(memory_space=pltpu.VMEM)
    anywhere = pl.BlockSpec(memory_space=pl.ANY)
    V = pltpu.VMEM
    dma = pltpu.SemaphoreType.DMA
    scratch = [
        V((D, HALF), BF), V((D, HALF), BF), V((HALF, D), BF),
        V((512, PIECE), BF), V((512, PIECE), BF), V((512, PIECE), BF), V((16, Q * TOK), F32),
        V((WIRE, PIECE), BF), V((WIRE, PIECE), BF), V((WIRE, PIECE), BF),
        V((WIRE, PIECE), BF), V((WIRE, PIECE), BF), V((WIRE, PIECE), BF),
        V((2 * ROWS, D), BF), V((ROWS, HALF), BF), V((ROWS, HALF), BF), V((2 * ROWS, HALF), BF), V((2 * ROWS, 128), BF),
        V((ROWS, D), BF), V((ROWS, D), BF), V((ROWS, D), BF),
        V((WIRE, PIECE), BF), V((WIRE, PIECE), BF),
        V((WIRE, PART), BF), V((S * 48, PART), BF),
        V((EXPERTS * 16, 128), BF), V((EXPERTS * 16, 128), BF),
        V((2 * S * TOK, WIRE), BF), V((1024, WIRE), BF),
        V((256, PIECE), F32), V((256, PIECE), BF), V((256, PIECE), BF),
        V((256, 128), F32), V((128, 128), BF), V((128, 128), BF),
        V((EXPERTS * TOK, 128), BF), V((EXPERTS * TOK, LATENT), BF), V((128, LATENT), F32), V((KV_ROWS, LATENT), F32),
        V((TOK, D), BF), V((TOK, D), BF), V((TOK, D), BF), V((TOK, D), BF),
        dma((3,)), dma((7,)), dma((7,)), dma((8, 31)), dma((8, 31)), dma((8,)), dma((2,)), dma((2,)),
    ]
    fwd, bwd, kv = pl.pallas_call(
        kernel,
        out_shape=[
            jax.ShapeDtypeStruct((TOK, D), BF),
            jax.ShapeDtypeStruct((TOK, D), BF),
            jax.ShapeDtypeStruct((KV_ROWS, LATENT), F32),
        ],
        in_specs=[vmem] * 9 + [anywhere] * 5,
        out_specs=[vmem] * 3,
        scratch_shapes=scratch,
        compiler_params=pltpu.CompilerParams(collective_id=0, has_side_effects=True, vmem_limit_bytes=63 * 2**20),
        name="layer",
    )(
        x_fwd[0], x_bwd[0], cot_bwd[0], meta, router, *consts,
        gate_weight[0, 0], up_weight[0, 0], down_weight[0, 0], attn, latent_cot[0],
    )
    return fwd[None], bwd[None], kv[None]


def solution(mesh):
    tokens = P("pipe", ("dp", "expert"), None)
    in_specs = (
        tokens, tokens, tokens, tokens, tokens,
        P("pipe", None, None),
        P("pipe", "expert", None, "dp"),
        P("pipe", "expert", None, "dp"),
        P("pipe", "expert", "dp", None),
        tokens, tokens,
    )
    return jax.shard_map(body, mesh=mesh, in_specs=in_specs, out_specs=(tokens,) * 3, check_vma=False)
```

```python
import functools

import jax
import jax.numpy as jnp
import numpy as np
from jax import lax
from jax.experimental import pallas as pl
from jax.experimental.pallas import tpu as pltpu
from jax.sharding import PartitionSpec as P

TOP = 2
ROUTE_SCALE = 2.5
CAP = 6
TOK = 64
D = 3584
EXPERTS = 32
HALF = 512
LATENT = 512
Q = 4
PIECE = D // Q
S = 7
PART = D // S
SLOT = 2 * CAP * Q
WIRE = EXPERTS * SLOT
ROWS = EXPERTS * CAP
CHUNK = 8
KV_ROWS = 56
MESH = pl.DeviceIdType.MESH
BF = jnp.bfloat16
F32 = jnp.float32

STEPS = [(2, 2), (1, 0), (3, 0), (0, 1), (0, 3), (2, 0), (0, 2), (1, 1), (3, 3), (1, 3), (3, 1), (2, 1), (1, 2), (2, 3), (3, 2)]
STEPS_X = sum(x * 4**i for i, (x, _) in enumerate(STEPS))
STEPS_Y = sum(y * 4**i for i, (_, y) in enumerate(STEPS))


def permutations():
    unpack = np.zeros((CHUNK * SLOT, CHUNK * SLOT), np.float32)
    pack_part = np.zeros((CHUNK * SLOT, S * CHUNK * CAP), np.float32)
    pack_inner = np.zeros((EXPERTS * 16, ROWS), np.float32)
    for s in range(CHUNK):
        for slot in range(CAP):
            for q in range(Q):
                for j in range(2):
                    unpack[j * 192 + q * 48 + s * CAP + slot, s * SLOT + q * 12 + j * CAP + slot] = 1
            for q in range(S):
                pack_part[s * SLOT + q * CAP + slot, q * 48 + s * CAP + slot] = 1
    for s in range(EXPERTS):
        for slot in range(CAP):
            pack_inner[s * 16 + slot, s * CAP + slot] = 1
    return unpack, unpack.T.copy(), pack_part, pack_inner


def dot(a, b):
    return jnp.dot(a, b, preferred_element_type=F32)


def dot_nt(a, b):
    return lax.dot_general(a, b, (((1,), (1,)), ((), ())), preferred_element_type=F32)


def kernel(
    xf, xb, cg, routes_f, routes_b, attn, latent, router, unpack, pack, pack_part, pack_inner,
    gate_hbm, up_hbm, down_hbm,
    fwd_out, bwd_out, kv_out,
    gate, up, down, stack_f, stack_own, stack_peer, meta, meta_peer, cols_own, cols_peer,
    w1, w2, a1, a2, a3, x2, gg, gu, hid, inner, inner_got, inner_sum,
    back_own, back_peer, back_got, fwd_rows, a4, a5, part,
    iv_wire, iv_got, g_part, g_pair, acc, peer_part, peer_got,
    attn_wire, attn_got, latent_got, kv_sum, kv_got, y_send, dx_send, y_got, dx_got,
    load_sem, z_send, z_recv, u_send, u_recv, local_sem, l_send, l_recv, p_send, p_recv,
):
    pi, dp, ex = lax.axis_index("pipe"), lax.axis_index("dp"), lax.axis_index("expert")
    core = lax.rem(ex, 2)
    px = lax.rem(lax.div(ex, 2), 4)
    py = lax.div(ex, 8)
    zpeer = (pi, 1 - dp, ex)
    ahead = (lax.rem(pi + 1, 4), dp, ex)
    behind = (lax.rem(pi + 3, 4), dp, ex)

    loads = [
        pltpu.make_async_copy(src, dst, load_sem.at[i])
        for i, (src, dst) in enumerate([(gate_hbm, gate), (up_hbm, up), (down_hbm, down)])
    ]

    barrier = pltpu.get_barrier_semaphore()
    pl.semaphore_signal(barrier, inc=1, device_id=zpeer, device_id_type=MESH)
    pl.semaphore_signal(barrier, inc=1, device_id=ahead, device_id_type=MESH)
    pl.semaphore_signal(barrier, inc=1, device_id=behind, device_id_type=MESH)

    def greet(o, c):
        pl.semaphore_signal(barrier, inc=1, device_id=(pi, dp, lax.rem(ex + o, EXPERTS)), device_id_type=MESH)
        return c

    lax.fori_loop(1, EXPERTS, greet, 0)
    for load in loads:
        load.start()

    def plane(unit, src, dst, rows, place_at, cols=None):
        def piece(e):
            at = pl.ds(pl.multiple_of(e * rows, 16), rows)
            return src.at[at] if cols is None else src.at[at, pl.ds(0, cols)]

        def copy(i, dx, dy, dc):
            to = (lax.rem(py + dy, 4) * 4 + lax.rem(px + dx, 4)) * 2 + lax.rem(core + dc, 2)
            return pltpu.make_async_remote_copy(
                src_ref=piece(to),
                dst_ref=dst.at[pl.ds(pl.multiple_of(place_at * rows, 16), rows)],
                send_sem=u_send.at[unit, i],
                recv_sem=u_recv.at[unit, i],
                device_id=(pi, dp, to),
                device_id_type=MESH,
            )

        def local():
            return pltpu.make_async_copy(
                piece(ex),
                dst.at[pl.ds(pl.multiple_of(place_at * rows, 16), rows)],
                local_sem.at[unit],
            )

        def start():
            def step(i, c):
                tx, ty = c
                dx, dy = lax.rem(tx, 4), lax.rem(ty, 4)
                copy(2 * i, dx, dy, 0).start()
                copy(2 * i + 1, dx, dy, 1).start()
                return lax.div(tx, 4), lax.div(ty, 4)

            lax.fori_loop(0, 15, step, (jnp.int32(STEPS_X), jnp.int32(STEPS_Y)))
            copy(30, 0, 0, 1).start()
            local().start()

        def wait_recv():
            def step(i, c):
                pltpu.make_async_copy(dst.at[pl.ds(0, rows)], dst.at[pl.ds(0, rows)], u_recv.at[unit, i]).wait()
                return c

            lax.fori_loop(0, 31, step, 0)
            local().wait()

        def wait_send():
            def step(i, c):
                pltpu.make_async_copy(dst.at[pl.ds(0, rows)], dst.at[pl.ds(0, rows)], u_send.at[unit, i]).wait()
                return c

            lax.fori_loop(0, 31, step, 0)

        return start, wait_recv, wait_send

    def to_zpeer(i, src, dst):
        return pltpu.make_async_remote_copy(
            src_ref=src, dst_ref=dst, send_sem=z_send.at[i], recv_sem=z_recv.at[i], device_id=zpeer, device_id_type=MESH
        )

    def place(code_a, code_b, stack, wire):
        first = jnp.concatenate([code_a[0:1], code_b[0:1] + float(CAP)], axis=1).astype(jnp.int32)
        second = jnp.concatenate([code_a[1:2], code_b[1:2] + float(CAP)], axis=1).astype(jnp.int32)

        def step(g, c):
            row = lax.broadcasted_iota(jnp.int32, (192, 512), 0) + g * 192
            member = jnp.where((row == first) | (row == second), 1.0, 0.0).astype(BF)
            wire[pl.ds(pl.multiple_of(g * 192, 16), 192), :] = dot(member, stack[...]).astype(BF)
            return c

        lax.fori_loop(0, 8, step, 0)

    def unpacked(wire):
        def step(c, carry):
            rows = dot(unpack[...], wire[pl.ds(pl.multiple_of(c * 384, 16), 384), :]).astype(BF)
            for j in range(2):
                for q in range(Q):
                    x2[pl.ds(pl.multiple_of(j * ROWS + c * 48, 16), 48), q * PIECE : (q + 1) * PIECE] = rows[
                        j * 192 + q * 48 : j * 192 + (q + 1) * 48
                    ]
            return carry

        lax.fori_loop(0, 4, step, 0)

    lane = lax.broadcasted_iota(jnp.int32, (TOK, 128), 1)

    def columns(values):
        out = jnp.zeros((TOK, 128), F32)
        for i, v in enumerate(values):
            out = jnp.where(lane == i, v, out)
        return out

    same_token = lax.broadcasted_iota(jnp.int32, (TOK, Q * TOK), 1) & (TOK - 1)
    same_token = jnp.where(same_token == lax.broadcasted_iota(jnp.int32, (TOK, Q * TOK), 0), 1.0, 0.0).astype(BF)
    named, named_rows = [], []
    for routes in (routes_f, routes_b):
        values = routes[...].astype(F32).astype(BF)
        turned = dot_nt(same_token[:, 0:TOK], values)
        tiled = dot(values, same_token)
        for k in range(TOP):
            named.append(turned[:, k : k + 1])
            named_rows.append(tiled[k : k + 1])
    lane_q = lax.broadcasted_iota(jnp.int32, (TOK, Q * TOK), 1)
    before = lax.broadcasted_iota(jnp.int32, (TOK, Q * TOK), 0) < (lane_q & (TOK - 1))
    offset = ((lane_q[0:1] >> 6) * 12).astype(F32)
    for i in range(4):
        row = named_rows[i]
        same = (named[i // 2 * 2] == row) | (named[i // 2 * 2 + 1] == row)
        slot = jnp.sum(jnp.where(same & before, 1.0, 0.0), axis=0, keepdims=True)
        meta[i : i + 1, :] = row * float(SLOT) + slot + offset
        if i >= 2:
            meta[i + 2 : i + 3, :] = row * 16.0 + slot
            meta[i + 4 : i + 5, :] = row

    for q in range(Q):
        cols = slice(q * PIECE, (q + 1) * PIECE)
        stack_f[q * TOK : (q + 1) * TOK, :] = xf[:, cols]
        stack_own[q * TOK : (q + 1) * TOK, :] = xb[:, cols]
        stack_own[256 + q * TOK : 256 + (q + 1) * TOK, :] = cg[:, cols]
    own = meta[...]
    place(own[2:4], own[2:4], stack_own, w1)
    group = (core * 4 + py) * 4
    latent_at = pl.ds(pl.multiple_of((group + px) * TOK, 16), TOK)
    latent_got[latent_at, :] = latent[...]

    pl.semaphore_wait(barrier, 34)
    z_meta = to_zpeer(0, meta, meta_peer)
    z_xg = to_zpeer(1, stack_own, stack_peer)
    z_f = to_zpeer(2, stack_f.at[pl.ds(0, 256)], stack_f.at[pl.ds(256, 256)])
    z_cols = to_zpeer(3, cols_own, cols_peer)
    z_meta.start()
    z_xg.start()
    start1, recv1, sent1 = plane(0, w1, a1, SLOT, ex)
    start1()

    def latent_copy(i, at, device):
        return pltpu.make_async_remote_copy(
            src_ref=latent_got.at[at], dst_ref=latent_got.at[at], send_sem=l_send.at[i], recv_sem=l_recv.at[i],
            device_id=(pi, dp, device), device_id_type=MESH,
        )

    along_x = [latent_copy(i, latent_at, (py * 4 + lax.rem(px + 1 + i, 4)) * 2 + core) for i in range(3)]
    row_at = pl.ds(pl.multiple_of(group * TOK, 16), 4 * TOK)
    along_y = [latent_copy(3 + i, row_at, (lax.rem(py + 1 + i, 4) * 4 + px) * 2 + core) for i in range(3)]
    core_at = pl.ds(pl.multiple_of(core * 16 * TOK, 16), 16 * TOK)
    to_core = latent_copy(6, core_at, ex + 1 - 2 * core)
    for c in along_x:
        c.start()

    lane_e = lax.broadcasted_iota(jnp.int32, (TOK, EXPERTS), 1)

    def rates_of(tokens, names):
        logits = dot_nt(tokens[...], router[...])
        return [
            jax.nn.sigmoid(jnp.sum(jnp.where(lane_e == e.astype(jnp.int32), logits, 0.0), axis=1, keepdims=True)) for e in names
        ]

    rate_f = rates_of(xf, named[0:2])
    rate_b = rates_of(xb, named[2:4])
    total_f, total_b = rate_f[0] + rate_f[1], rate_b[0] + rate_b[1]
    gate_f = [ROUTE_SCALE * r / total_f for r in rate_f]
    gate_b = [ROUTE_SCALE * r / total_b for r in rate_b]
    cols_own[...] = columns(gate_f + gate_b + rate_b + [total_b])
    z_cols.start()

    for e in range(EXPERTS):
        halves = []
        for h in range(2):
            first = h * (D // 2) + e * KV_ROWS
            start = min(first // 128 * 128, D - 256)
            window = attn[:, start : start + 256].astype(F32)
            halves.append(pltpu.roll(window, (256 - (first - start) + h * 64) % 256, 1)[:, 0:128])
        attn_wire[e * TOK : (e + 1) * TOK, :] = jnp.where(lane < 64, halves[0], halves[1]).astype(BF)

    z_meta.wait_recv()
    peer = meta_peer[...]
    own_t, peer_t = own.T, peer.T

    def split(values):
        hi = values.astype(BF)
        return hi, (values - hi.astype(F32)).astype(BF)

    lane_w = lax.broadcasted_iota(jnp.int32, (TOK, WIRE), 1)

    def gate_rows(code0, code1, gate0, gate1, offset):
        value = jnp.where(lane_w == code0.astype(jnp.int32) + offset, gate0, 0.0)
        value = value + jnp.where(lane_w == code1.astype(jnp.int32) + offset, gate1, 0.0)
        return split(value)

    def forward_gates(j, m, gates):
        for q in range(Q):
            m_q = m[q * TOK : (q + 1) * TOK]
            hi, lo = gate_rows(m_q[:, 0:1], m_q[:, 1:2], gates[:, 0:1], gates[:, 1:2], j * CAP)
            g_pair[j * 512 + q * TOK : j * 512 + (q + 1) * TOK, :] = hi
            g_pair[j * 512 + 256 + q * TOK : j * 512 + 256 + (q + 1) * TOK, :] = lo

    forward_gates(0, own_t, cols_own[...])
    for q in range(S):
        m = own_t[0:TOK]
        hi, lo = gate_rows(m[:, 2:3], m[:, 3:4], cols_own[:, 2:3], cols_own[:, 3:4], q * CAP)
        g_part[q * TOK : (q + 1) * TOK, :] = hi
        g_part[S * TOK + q * TOK : S * TOK + (q + 1) * TOK, :] = lo
    for c in along_x:
        c.wait_recv()
    for c in along_y:
        c.start()

    z_xg.wait_recv()
    z_f.start()
    place(peer[2:4], peer[2:4], stack_peer, w2)
    start2, recv2, sent2 = plane(1, w2, a2, SLOT, ex)
    start2()

    def backward(rows_out, after=None):
        total = jnp.zeros((ROWS, 1), F32)
        for n in range(HALF // 256):
            cols = slice(n * 256, (n + 1) * 256)
            gate_act = dot(x2[0:ROWS, :], gate[:, cols])
            up_act = dot(x2[0:ROWS, :], up[:, cols])
            grad_hidden = dot_nt(x2[ROWS : 2 * ROWS, :], down[cols, :])
            sig = jax.nn.sigmoid(gate_act)
            active = gate_act * sig
            hidden = (active * up_act).astype(BF).astype(F32)
            total = total + jnp.sum(hidden * grad_hidden, axis=1, keepdims=True)
            gg[:, cols] = (grad_hidden * up_act * sig * (1.0 + gate_act * (1.0 - sig))).astype(BF)
            gu[:, cols] = (grad_hidden * active).astype(BF)
        for q in range(Q):
            cols = slice(q * PIECE, (q + 1) * PIECE)
            rows_out[:, cols] = (dot_nt(gg[...], gate[cols, :]) + dot_nt(gu[...], up[cols, :])).astype(BF)
            if after is not None:
                after[q].start()
        return total

    side = lax.broadcasted_iota(jnp.int32, (ROWS, 128), 1) < 64

    def hi_lo(total):
        hi, lo = split(total)
        return jnp.where(side, hi.astype(F32), lo.astype(F32)).astype(BF)

    for load in loads:
        load.wait()
    recv1()
    unpacked(a1)
    inner[0:ROWS, :] = hi_lo(backward(back_own))

    z_f.wait_recv()
    sent1()
    place(own[0:2], peer[0:2], stack_f, w1)
    start3, recv3, sent3 = plane(2, w1, a3, SLOT, ex)
    start3()
    for c in along_y:
        c.wait_recv()
    to_core.start()
    z_cols.wait_recv()
    forward_gates(1, peer_t, cols_peer[...])

    q_cols = [pl.ds(q * PIECE, PIECE) for q in range(Q)]
    z_back = [to_zpeer(4 + q, back_peer.at[:, q_cols[q]], back_got.at[:, q_cols[q]]) for q in range(Q)]
    z_inner = to_zpeer(8, inner.at[pl.ds(ROWS, ROWS)], inner_got)
    recv2()
    unpacked(a2)
    inner[ROWS : 2 * ROWS, :] = hi_lo(backward(back_peer, z_back))
    z_inner.start()

    recv3()
    start_a, recv_a, sent_a = plane(5, attn_wire, attn_got, TOK, group + px)
    start_a()
    unpacked(a3)
    for n in range(HALF // 256):
        cols = slice(n * 256, (n + 1) * 256)
        gate_act = dot(x2[...], gate[:, cols])
        up_act = dot(x2[...], up[:, cols])
        hid[:, cols] = (gate_act * jax.nn.sigmoid(gate_act) * up_act).astype(BF)
    for q in range(Q):
        rows = dot(hid[...], down[:, q * PIECE : (q + 1) * PIECE]).astype(BF)
        for j in range(2):
            for g in range(4):
                at = g * 384 + j * 192 + q * 48
                fwd_rows[at : at + 48, :] = rows[j * ROWS + g * 48 : j * ROWS + (g + 1) * 48]
    sent2()

    def pack_forward(g, c):
        rows = pl.ds(pl.multiple_of(g * 384, 16), 384)
        w2[rows, :] = dot(pack[...], fwd_rows[rows, :]).astype(BF)
        return c

    lax.fori_loop(0, 4, pack_forward, 0)
    start4, recv4, sent4 = plane(3, w2, a4, SLOT, ex)
    start4()

    to_core.wait_recv()
    recv_a()
    kv_sum[...] = lax.dot_general(attn_got[...], latent_got[...], (((0,), (0,)), ((), ())), preferred_element_type=F32)
    z_kv = to_zpeer(9, kv_sum.at[pl.ds(pl.multiple_of((1 - dp) * 64, 8), KV_ROWS)], kv_got)
    z_kv.start()

    z_inner.wait_recv()
    total = inner[0:ROWS, :].astype(F32) + inner_got[...].astype(F32)
    inner_sum[...] = hi_lo(total[:, 0:1] + total[:, 64:65])
    iv_wire[...] = dot(pack_inner[...], inner_sum[...]).astype(BF)
    start_i, recv_i, sent_i = plane(4, iv_wire, iv_got, 16, ex)
    start_i()
    for c in z_back:
        c.wait_recv()
    sent3()

    def pack_back(g, c):
        rows = pl.ds(pl.multiple_of(g * 48, 16), 48)
        for q in range(S):
            cols = slice(q * PART, (q + 1) * PART)
            part[q * 48 : (q + 1) * 48, :] = (back_own[rows, cols].astype(F32) + back_got[rows, cols].astype(F32)).astype(BF)
        w1[pl.ds(pl.multiple_of(g * 384, 16), 384), 0:PART] = dot(pack_part[...], part[...]).astype(BF)
        return c

    lax.fori_loop(0, 4, pack_back, 0)
    start5, recv5, sent5 = plane(6, w1, a5, SLOT, ex, cols=PART)
    start5()
    z_kv.wait_recv()
    kv_out[...] = kv_sum[pl.ds(pl.multiple_of(dp * 64, 8), KV_ROWS), :] + kv_got[...]

    recv4()
    got = dot(g_pair[512:1024, :], a4[...])
    peer_part[...] = (got[0:256] + got[256:512]).astype(BF)
    q_rows = [pl.ds(q * TOK, TOK) for q in range(Q)]
    z_part = [to_zpeer(10 + q, peer_part.at[q_rows[q]], peer_got.at[q_rows[q]]) for q in range(Q)]
    for c in z_part:
        c.start()
    got = dot(g_pair[0:512, :], a4[...])
    acc[...] = got[0:256] + got[256:512]
    for q in range(Q):
        rows = slice(q * TOK, (q + 1) * TOK)
        acc[rows, :] = acc[rows, :] + xf[:, q * PIECE : (q + 1) * PIECE].astype(F32)

    recv_i()
    lane_i = lax.broadcasted_iota(jnp.int32, (TOK, EXPERTS * 16), 1)
    picks = [jnp.where(lane_i == own_t[0:TOK, 4 + k : 5 + k].astype(jnp.int32), 1.0, 0.0).astype(BF) for k in range(TOP)]
    val = dot(jnp.concatenate(picks, axis=0), iv_got[...])
    inner0 = val[0:64, 0:1] + val[0:64, 64:65]
    inner1 = val[64:128, 0:1] + val[64:128, 64:65]
    rate0, rate1, rate_total = cols_own[:, 4:5], cols_own[:, 5:6], cols_own[:, 6:7]
    weighted = (inner0 * rate0 + inner1 * rate1) / (rate_total * rate_total)
    logit0 = ROUTE_SCALE * (inner0 / rate_total - weighted) * rate0 * (1.0 - rate0)
    logit1 = ROUTE_SCALE * (inner1 / rate_total - weighted) * rate1 * (1.0 - rate1)
    dlogits = jnp.where(lane_e == named[2].astype(jnp.int32), logit0, 0.0)
    dlogits = (dlogits + jnp.where(lane_e == named[3].astype(jnp.int32), logit1, 0.0)).astype(BF)
    rest = dot(dlogits, router[...]) + cg[...].astype(F32)

    def to_next(i, src, dst):
        return pltpu.make_async_remote_copy(
            src_ref=src, dst_ref=dst, send_sem=p_send.at[i], recv_sem=p_recv.at[i], device_id=ahead, device_id_type=MESH
        )

    n_y = [to_next(q, y_send.at[q_rows[q]], y_got.at[q_rows[q]]) for q in range(Q)]
    for q in range(Q):
        rows = slice(q * TOK, (q + 1) * TOK)
        z_part[q].wait_recv()
        y_send[rows, :] = (acc[rows, :] + peer_got[rows, :].astype(F32)).astype(BF)
        n_y[q].start()

    recv5()
    got = dot(g_part[...], a5[...])
    for q in range(S):
        cols = slice(q * PART, (q + 1) * PART)
        dx = rest[:, cols] + got[q * TOK : (q + 1) * TOK] + got[(S + q) * TOK : (S + q + 1) * TOK]
        dx_send[:, cols] = dx.astype(BF)
    n_dx = to_next(4, dx_send, dx_got)
    n_dx.start()

    for q in range(Q):
        n_y[q].wait_recv()
        fwd_out[:, q * PIECE : (q + 1) * PIECE] = y_got[q * TOK : (q + 1) * TOK, :]
    n_dx.wait_recv()
    bwd_out[...] = dx_got[...]

    for sent in (sent4, sent_i, sent5, sent_a):
        sent()
    for copy in [z_meta, z_f, z_xg, z_cols, z_inner, z_kv, n_dx, to_core] + z_back + z_part + n_y + along_x + along_y:
        copy.wait_send()


def body(x_fwd, routes_fwd, x_bwd, cot_bwd, routes_bwd, router_weight, gate_weight, up_weight, down_weight, attn_input, latent_cot):
    consts = [jnp.asarray(c, BF) for c in permutations()]
    vmem = pl.BlockSpec(memory_space=pltpu.VMEM)
    anywhere = pl.BlockSpec(memory_space=pl.ANY)
    V = pltpu.VMEM
    dma = pltpu.SemaphoreType.DMA
    scratch = [
        V((D, HALF), BF), V((D, HALF), BF), V((HALF, D), BF),
        V((512, PIECE), BF), V((512, PIECE), BF), V((512, PIECE), BF),
        V((8, Q * TOK), F32), V((8, Q * TOK), F32), V((TOK, 128), F32), V((TOK, 128), F32),
        V((WIRE, PIECE), BF), V((WIRE, PIECE), BF),
        V((WIRE, PIECE), BF), V((WIRE, PIECE), BF), V((WIRE, PIECE), BF),
        V((2 * ROWS, D), BF), V((ROWS, HALF), BF), V((ROWS, HALF), BF), V((2 * ROWS, HALF), BF),
        V((2 * ROWS, 128), BF), V((ROWS, 128), BF), V((ROWS, 128), BF),
        V((ROWS, D), BF), V((ROWS, D), BF), V((ROWS, D), BF),
        V((WIRE, PIECE), BF), V((WIRE, PIECE), BF),
        V((WIRE, PART), BF), V((S * 48, PART), BF),
        V((EXPERTS * 16, 128), BF), V((EXPERTS * 16, 128), BF),
        V((2 * S * TOK, WIRE), BF), V((1024, WIRE), BF),
        V((256, PIECE), F32), V((256, PIECE), BF), V((256, PIECE), BF),
        V((EXPERTS * TOK, 128), BF), V((EXPERTS * TOK, 128), BF), V((EXPERTS * TOK, LATENT), BF), V((128, LATENT), F32), V((KV_ROWS, LATENT), F32),
        V((256, PIECE), BF), V((TOK, D), BF), V((256, PIECE), BF), V((TOK, D), BF),
        dma((3,)), dma((14,)), dma((14,)), dma((7, 31)), dma((7, 31)), dma((7,)), dma((7,)), dma((7,)), dma((5,)), dma((5,)),
    ]
    fwd, bwd, kv = pl.pallas_call(
        kernel,
        out_shape=[
            jax.ShapeDtypeStruct((TOK, D), BF),
            jax.ShapeDtypeStruct((TOK, D), BF),
            jax.ShapeDtypeStruct((KV_ROWS, LATENT), F32),
        ],
        in_specs=[vmem] * 12 + [anywhere] * 3,
        out_specs=[vmem] * 3,
        scratch_shapes=scratch,
        compiler_params=pltpu.CompilerParams(collective_id=0, has_side_effects=True, vmem_limit_bytes=63 * 2**20),
        name="layer",
    )(
        x_fwd[0], x_bwd[0], cot_bwd[0], routes_fwd[0].T, routes_bwd[0].T, attn_input[0], latent_cot[0], router_weight[0].T, *consts,
        gate_weight[0, 0], up_weight[0, 0], down_weight[0, 0],
    )
    return fwd[None], bwd[None], kv[None]


def solution(mesh):
    tokens = P("pipe", ("dp", "expert"), None)
    in_specs = (
        tokens, tokens, tokens, tokens, tokens,
        P("pipe", None, None),
        P("pipe", "expert", None, "dp"),
        P("pipe", "expert", None, "dp"),
        P("pipe", "expert", "dp", None),
        tokens, tokens,
    )
    return jax.shard_map(body, mesh=mesh, in_specs=in_specs, out_specs=(tokens,) * 3, check_vma=False)
```

```python
import functools

import jax
import jax.numpy as jnp
import numpy as np
from jax import lax
from jax.experimental import pallas as pl
from jax.experimental.pallas import tpu as pltpu
from jax.sharding import PartitionSpec as P

TOP = 2
ROUTE_SCALE = 2.5
CAP = 6
TOK = 64
D = 3584
EXPERTS = 32
HALF = 512
LATENT = 512
Q = 4
PIECE = D // Q
S = 7
PART = D // S
SLOT = 2 * CAP * Q
WIRE = EXPERTS * SLOT
ROWS = EXPERTS * CAP
CHUNK = 8
KV_ROWS = 56
LANES = ((0, 512), (512, PIECE))
MESH = pl.DeviceIdType.MESH
BF = jnp.bfloat16
F32 = jnp.float32

STEPS = [(2, 2), (1, 0), (3, 0), (0, 1), (0, 3), (2, 0), (0, 2), (1, 1), (3, 3), (1, 3), (3, 1), (2, 1), (1, 2), (2, 3), (3, 2)]
STEPS_X = sum(x * 4**i for i, (x, _) in enumerate(STEPS))
STEPS_Y = sum(y * 4**i for i, (_, y) in enumerate(STEPS))


def permutations():
    unpack = np.zeros((CHUNK * SLOT, CHUNK * SLOT), np.float32)
    pack_part = np.zeros((CHUNK * SLOT, S * CHUNK * CAP), np.float32)
    pack_inner = np.zeros((EXPERTS * 16, ROWS), np.float32)
    for s in range(CHUNK):
        for slot in range(CAP):
            for q in range(Q):
                for j in range(2):
                    unpack[j * 192 + q * 48 + s * CAP + slot, s * SLOT + q * 12 + j * CAP + slot] = 1
            for q in range(S):
                pack_part[s * SLOT + q * CAP + slot, q * 48 + s * CAP + slot] = 1
    for s in range(EXPERTS):
        for slot in range(CAP):
            pack_inner[s * 16 + slot, s * CAP + slot] = 1
    return unpack, unpack.T.copy(), pack_part, pack_inner


def dot(a, b):
    return jnp.dot(a, b, preferred_element_type=F32)


def dot_nt(a, b):
    return lax.dot_general(a, b, (((1,), (1,)), ((), ())), preferred_element_type=F32)


def kernel(
    xf, xb, cg, routes_f, routes_b, attn, latent, router, unpack, pack, pack_part, pack_inner,
    gate_hbm, up_hbm, down_hbm,
    fwd_out, bwd_out, kv_out,
    gate, up, down, stack1, stack2, stack3, meta, meta_peer, cols_own, cols_peer,
    w1, w2, a1, a2, a3, x2, x_own, gg, gu, hid, inner, inner_got, inner_sum,
    back_own, back_peer, back_got, fwd_rows, a4, a5, part,
    iv_wire, iv_got, g_part, g_pair, acc, peer_part, peer_got,
    attn_wire, attn_got, latent_got, kv_sum, kv_got, y_send, dx_send, y_got, dx_got,
    load_sem, z_send, z_recv, u_send, u_recv, local_sem, l_send, l_recv, p_send, p_recv,
):
    pi, dp, ex = lax.axis_index("pipe"), lax.axis_index("dp"), lax.axis_index("expert")
    core = lax.rem(ex, 2)
    px = lax.rem(lax.div(ex, 2), 4)
    py = lax.div(ex, 8)
    zpeer = (pi, 1 - dp, ex)
    ahead = (lax.rem(pi + 1, 4), dp, ex)
    behind = (lax.rem(pi + 3, 4), dp, ex)

    loads = [
        pltpu.make_async_copy(src, dst, load_sem.at[i])
        for i, (src, dst) in enumerate([(gate_hbm, gate), (up_hbm, up), (down_hbm, down)])
    ]

    barrier = pltpu.get_barrier_semaphore()
    pl.semaphore_signal(barrier, inc=1, device_id=zpeer, device_id_type=MESH)
    pl.semaphore_signal(barrier, inc=1, device_id=ahead, device_id_type=MESH)
    pl.semaphore_signal(barrier, inc=1, device_id=behind, device_id_type=MESH)

    def greet(o, c):
        pl.semaphore_signal(barrier, inc=1, device_id=(pi, dp, lax.rem(ex + o, EXPERTS)), device_id_type=MESH)
        return c

    lax.fori_loop(1, EXPERTS, greet, 0)
    for load in loads:
        load.start()

    def plane(unit, src, dst, rows, place_at, lanes=None, land=None):
        def piece(e):
            at = pl.ds(pl.multiple_of(e * rows, 16), rows)
            return src.at[at] if lanes is None else src.at[at, lanes]

        landing = pl.ds(pl.multiple_of(place_at * rows, 16), rows)
        landing = dst.at[landing] if land is None else dst.at[landing, land]
        sample = dst.at[pl.ds(0, rows)] if land is None else dst.at[pl.ds(0, rows), land]

        def copy(i, dx, dy, dc):
            to = (lax.rem(py + dy, 4) * 4 + lax.rem(px + dx, 4)) * 2 + lax.rem(core + dc, 2)
            return pltpu.make_async_remote_copy(
                src_ref=piece(to),
                dst_ref=landing,
                send_sem=u_send.at[unit, i],
                recv_sem=u_recv.at[unit, i],
                device_id=(pi, dp, to),
                device_id_type=MESH,
            )

        def local():
            return pltpu.make_async_copy(
                piece(ex),
                landing,
                local_sem.at[unit],
            )

        def start():
            def step(i, c):
                tx, ty = c
                dx, dy = lax.rem(tx, 4), lax.rem(ty, 4)
                copy(2 * i, dx, dy, 0).start()
                copy(2 * i + 1, dx, dy, 1).start()
                return lax.div(tx, 4), lax.div(ty, 4)

            lax.fori_loop(0, 15, step, (jnp.int32(STEPS_X), jnp.int32(STEPS_Y)))
            copy(30, 0, 0, 1).start()
            local().start()

        def wait_recv():
            def step(i, c):
                pltpu.make_async_copy(sample, sample, u_recv.at[unit, i]).wait()
                return c

            lax.fori_loop(0, 31, step, 0)
            local().wait()

        def wait_send():
            def step(i, c):
                pltpu.make_async_copy(sample, sample, u_send.at[unit, i]).wait()
                return c

            lax.fori_loop(0, 31, step, 0)

        return start, wait_recv, wait_send

    def to_zpeer(i, src, dst):
        return pltpu.make_async_remote_copy(
            src_ref=src, dst_ref=dst, send_sem=z_send.at[i], recv_sem=z_recv.at[i], device_id=zpeer, device_id_type=MESH
        )

    def place(code_a, code_b, stack, wire, low=0, high=PIECE):
        first = jnp.concatenate([code_a[0:1], code_b[0:1] + float(CAP)], axis=1).astype(jnp.int32)
        second = jnp.concatenate([code_a[1:2], code_b[1:2] + float(CAP)], axis=1).astype(jnp.int32)

        def step(g, c):
            row = lax.broadcasted_iota(jnp.int32, (192, 512), 0) + g * 192
            member = jnp.where((row == first) | (row == second), 1.0, 0.0).astype(BF)
            wire[pl.ds(pl.multiple_of(g * 192, 16), 192), low:high] = dot(member, stack[:, low:high]).astype(BF)
            return c

        lax.fori_loop(0, 8, step, 0)

    def unpacked(wire, *targets):
        def step(c, carry):
            rows = dot(unpack[...], wire[pl.ds(pl.multiple_of(c * 384, 16), 384), :]).astype(BF)
            at = pl.ds(pl.multiple_of(c * 48, 16), 48)
            for j in range(2):
                for q in range(Q):
                    targets[j][at, q * PIECE : (q + 1) * PIECE] = rows[j * 192 + q * 48 : j * 192 + (q + 1) * 48]
            return carry

        lax.fori_loop(0, 4, step, 0)

    x_rows, g_rows = x2.at[pl.ds(0, ROWS)], x2.at[pl.ds(ROWS, ROWS)]

    lane = lax.broadcasted_iota(jnp.int32, (TOK, 128), 1)

    def columns(values):
        out = jnp.zeros((TOK, 128), F32)
        for i, v in enumerate(values):
            out = jnp.where(lane == i, v, out)
        return out

    same_token = lax.broadcasted_iota(jnp.int32, (TOK, Q * TOK), 1) & (TOK - 1)
    same_token = jnp.where(same_token == lax.broadcasted_iota(jnp.int32, (TOK, Q * TOK), 0), 1.0, 0.0).astype(BF)
    named, named_rows = [], []
    for routes in (routes_f, routes_b):
        values = routes[...].astype(F32).astype(BF)
        turned = dot_nt(same_token[:, 0:TOK], values)
        tiled = dot(values, same_token)
        for k in range(TOP):
            named.append(turned[:, k : k + 1])
            named_rows.append(tiled[k : k + 1])
    lane_q = lax.broadcasted_iota(jnp.int32, (TOK, Q * TOK), 1)
    before = lax.broadcasted_iota(jnp.int32, (TOK, Q * TOK), 0) < (lane_q & (TOK - 1))
    offset = ((lane_q[0:1] >> 6) * 12).astype(F32)
    for i in range(4):
        row = named_rows[i]
        same = (named[i // 2 * 2] == row) | (named[i // 2 * 2 + 1] == row)
        slot = jnp.sum(jnp.where(same & before, 1.0, 0.0), axis=0, keepdims=True)
        meta[i : i + 1, :] = row * float(SLOT) + slot + offset
        if i >= 2:
            meta[i + 2 : i + 3, :] = row * 16.0 + slot
            meta[i + 4 : i + 5, :] = row

    for q in range(Q):
        cols = slice(q * PIECE, (q + 1) * PIECE)
        stack1[q * TOK : (q + 1) * TOK, :] = xf[:, cols]
        stack1[256 + q * TOK : 256 + (q + 1) * TOK, :] = xb[:, cols]
        stack3[q * TOK : (q + 1) * TOK, :] = cg[:, cols]
    own = meta[...]
    place(own[0:2], own[2:4], stack1, w1)
    group = (core * 4 + py) * 4
    latent_at = pl.ds(pl.multiple_of((group + px) * TOK, 16), TOK)
    latent_got[latent_at, :] = latent[...]

    pl.semaphore_wait(barrier, 34)
    z_meta = to_zpeer(0, meta, meta_peer)
    top, bottom = pl.ds(0, 256), pl.ds(256, 256)
    z_xg = []
    for i, (low, high) in enumerate(LANES):
        lanes = pl.ds(low, high - low)
        z_xg.append(to_zpeer(14 + 2 * i, stack1.at[bottom, lanes], stack2.at[top, lanes]))
        z_xg.append(to_zpeer(15 + 2 * i, stack3.at[top, lanes], stack2.at[bottom, lanes]))
    z_f = to_zpeer(2, stack1.at[top], stack3.at[bottom])
    z_cols = to_zpeer(3, cols_own, cols_peer)
    z_meta.start()
    z_xg[0].start()
    z_xg[1].start()
    start1, recv1, sent1 = plane(0, w1, a1, SLOT, ex)
    start1()

    def latent_copy(i, at, device):
        return pltpu.make_async_remote_copy(
            src_ref=latent_got.at[at], dst_ref=latent_got.at[at], send_sem=l_send.at[i], recv_sem=l_recv.at[i],
            device_id=(pi, dp, device), device_id_type=MESH,
        )

    along_x = [latent_copy(i, latent_at, (py * 4 + lax.rem(px + 1 + i, 4)) * 2 + core) for i in range(3)]
    row_at = pl.ds(pl.multiple_of(group * TOK, 16), 4 * TOK)
    along_y = [latent_copy(3 + i, row_at, (lax.rem(py + 1 + i, 4) * 4 + px) * 2 + core) for i in range(3)]
    core_at = pl.ds(pl.multiple_of(core * 16 * TOK, 16), 16 * TOK)
    to_core = latent_copy(6, core_at, ex + 1 - 2 * core)
    for c in along_x:
        c.start()

    lane_e = lax.broadcasted_iota(jnp.int32, (TOK, EXPERTS), 1)

    def rates_of(tokens, names):
        logits = dot_nt(tokens[...], router[...])
        return [
            jax.nn.sigmoid(jnp.sum(jnp.where(lane_e == e.astype(jnp.int32), logits, 0.0), axis=1, keepdims=True)) for e in names
        ]

    rate_f = rates_of(xf, named[0:2])
    rate_b = rates_of(xb, named[2:4])
    total_f, total_b = rate_f[0] + rate_f[1], rate_b[0] + rate_b[1]
    gate_f = [ROUTE_SCALE * r / total_f for r in rate_f]
    gate_b = [ROUTE_SCALE * r / total_b for r in rate_b]
    cols_own[...] = columns(gate_f + gate_b + rate_b + [total_b])
    z_cols.start()

    for e in range(EXPERTS):
        halves = []
        for h in range(2):
            first = h * (D // 2) + e * KV_ROWS
            start = min(first // 128 * 128, D - 256)
            window = attn[:, start : start + 256].astype(F32)
            halves.append(pltpu.roll(window, (256 - (first - start) + h * 64) % 256, 1)[:, 0:128])
        attn_wire[e * TOK : (e + 1) * TOK, :] = jnp.where(lane < 64, halves[0], halves[1]).astype(BF)

    z_meta.wait_recv()
    peer = meta_peer[...]
    z_xg[0].wait_recv()
    z_xg[1].wait_recv()
    z_xg[2].start()
    z_xg[3].start()
    second = []
    for unit, (low, high) in zip((1, 7), LANES):
        lanes = pl.ds(low, high - low)
        second.append(plane(unit, w2, a2, SLOT, ex, lanes, lanes))
    place(peer[2:4], peer[2:4], stack2, w2, *LANES[0])
    second[0][0]()
    own_t, peer_t = own.T, peer.T

    def split(values):
        hi = values.astype(BF)
        return hi, (values - hi.astype(F32)).astype(BF)

    lane_w = lax.broadcasted_iota(jnp.int32, (TOK, WIRE), 1)

    def gate_rows(code0, code1, gate0, gate1, offset):
        value = jnp.where(lane_w == code0.astype(jnp.int32) + offset, gate0, 0.0)
        value = value + jnp.where(lane_w == code1.astype(jnp.int32) + offset, gate1, 0.0)
        return split(value)

    def forward_gates(j, m, gates):
        for q in range(Q):
            m_q = m[q * TOK : (q + 1) * TOK]
            hi, lo = gate_rows(m_q[:, 0:1], m_q[:, 1:2], gates[:, 0:1], gates[:, 1:2], j * CAP)
            g_pair[j * 512 + q * TOK : j * 512 + (q + 1) * TOK, :] = hi
            g_pair[j * 512 + 256 + q * TOK : j * 512 + 256 + (q + 1) * TOK, :] = lo

    forward_gates(0, own_t, cols_own[...])
    for q in range(S):
        m = own_t[0:TOK]
        hi, lo = gate_rows(m[:, 2:3], m[:, 3:4], cols_own[:, 2:3], cols_own[:, 3:4], q * CAP)
        g_part[q * TOK : (q + 1) * TOK, :] = hi
        g_part[S * TOK + q * TOK : S * TOK + (q + 1) * TOK, :] = lo
    for c in along_x:
        c.wait_recv()
    for c in along_y:
        c.start()

    z_xg[2].wait_recv()
    z_xg[3].wait_recv()
    z_f.start()
    place(peer[2:4], peer[2:4], stack2, w2, *LANES[1])
    second[1][0]()

    def backward(x, g, rows_out, after=None):
        total = jnp.zeros((ROWS, 1), F32)
        for n in range(HALF // 256):
            cols = slice(n * 256, (n + 1) * 256)
            gate_act = dot(x[...], gate[:, cols])
            up_act = dot(x[...], up[:, cols])
            grad_hidden = dot_nt(g[...], down[cols, :])
            sig = jax.nn.sigmoid(gate_act)
            active = gate_act * sig
            hidden = (active * up_act).astype(BF).astype(F32)
            total = total + jnp.sum(hidden * grad_hidden, axis=1, keepdims=True)
            gg[:, cols] = (grad_hidden * up_act * sig * (1.0 + gate_act * (1.0 - sig))).astype(BF)
            gu[:, cols] = (grad_hidden * active).astype(BF)
        for q in range(Q):
            cols = slice(q * PIECE, (q + 1) * PIECE)
            rows_out[:, cols] = (dot_nt(gg[...], gate[cols, :]) + dot_nt(gu[...], up[cols, :])).astype(BF)
            if after is not None:
                after[q].start()
        return total

    side = lax.broadcasted_iota(jnp.int32, (ROWS, 128), 1) < 64

    def hi_lo(total):
        hi, lo = split(total)
        return jnp.where(side, hi.astype(F32), lo.astype(F32)).astype(BF)

    def forward(j):
        for n in range(HALF // 256):
            cols = slice(n * 256, (n + 1) * 256)
            gate_act = dot(x_rows[...], gate[:, cols])
            up_act = dot(x_rows[...], up[:, cols])
            hid[:, cols] = (gate_act * jax.nn.sigmoid(gate_act) * up_act).astype(BF)
        for q in range(Q):
            rows = dot(hid[...], down[:, q * PIECE : (q + 1) * PIECE]).astype(BF)
            for g in range(4):
                at = g * 384 + j * 192 + q * 48
                fwd_rows[at : at + 48, :] = rows[g * 48 : (g + 1) * 48]

    for load in loads:
        load.wait()
    recv1()
    unpacked(a1, x_rows, x_own)
    forward(0)

    z_f.wait_recv()
    sent1()
    place(own[2:4], peer[0:2], stack3, w1)
    start3, recv3, sent3 = plane(2, w1, a3, SLOT, ex)
    start3()
    for c in along_y:
        c.wait_recv()
    to_core.start()
    z_cols.wait_recv()
    forward_gates(1, peer_t, cols_peer[...])

    q_cols = [pl.ds(q * PIECE, PIECE) for q in range(Q)]
    z_back = [to_zpeer(4 + q, back_peer.at[:, q_cols[q]], back_got.at[:, q_cols[q]]) for q in range(Q)]
    z_inner = to_zpeer(8, inner.at[pl.ds(ROWS, ROWS)], inner_got)
    for unit in second:
        unit[1]()
    unpacked(a2, x_rows, g_rows)
    inner[ROWS : 2 * ROWS, :] = hi_lo(backward(x_rows, g_rows, back_peer, z_back))
    z_inner.start()

    recv3()
    start_a, recv_a, sent_a = plane(5, attn_wire, attn_got, TOK, group + px)
    start_a()
    unpacked(a3, g_rows, x_rows)
    forward(1)
    for unit in second:
        unit[2]()

    def pack_forward(g, c):
        rows = pl.ds(pl.multiple_of(g * 384, 16), 384)
        w2[rows, :] = dot(pack[...], fwd_rows[rows, :]).astype(BF)
        return c

    lax.fori_loop(0, 4, pack_forward, 0)
    start4, recv4, sent4 = plane(3, w2, a4, SLOT, ex)
    start4()

    inner[0:ROWS, :] = hi_lo(backward(x_own, g_rows, back_own))

    to_core.wait_recv()
    recv_a()
    kv_sum[...] = lax.dot_general(attn_got[...], latent_got[...], (((0,), (0,)), ((), ())), preferred_element_type=F32)
    z_kv = to_zpeer(9, kv_sum.at[pl.ds(pl.multiple_of((1 - dp) * 64, 8), KV_ROWS)], kv_got)
    z_kv.start()

    z_inner.wait_recv()
    total = inner[0:ROWS, :].astype(F32) + inner_got[...].astype(F32)
    inner_sum[...] = hi_lo(total[:, 0:1] + total[:, 64:65])
    iv_wire[...] = dot(pack_inner[...], inner_sum[...]).astype(BF)
    start_i, recv_i, sent_i = plane(4, iv_wire, iv_got, 16, ex)
    start_i()
    for c in z_back:
        c.wait_recv()
    sent3()

    def pack_back(g, c):
        rows = pl.ds(pl.multiple_of(g * 48, 16), 48)
        for q in range(S):
            cols = slice(q * PART, (q + 1) * PART)
            part[q * 48 : (q + 1) * 48, :] = (back_own[rows, cols].astype(F32) + back_got[rows, cols].astype(F32)).astype(BF)
        w1[pl.ds(pl.multiple_of(g * 384, 16), 384), 0:PART] = dot(pack_part[...], part[...]).astype(BF)
        return c

    lax.fori_loop(0, 4, pack_back, 0)
    start5, recv5, sent5 = plane(6, w1, a5, SLOT, ex, pl.ds(0, PART))
    start5()
    z_kv.wait_recv()
    kv_out[...] = kv_sum[pl.ds(pl.multiple_of(dp * 64, 8), KV_ROWS), :] + kv_got[...]

    recv4()
    got = dot(g_pair[512:1024, :], a4[...])
    peer_part[...] = (got[0:256] + got[256:512]).astype(BF)
    q_rows = [pl.ds(q * TOK, TOK) for q in range(Q)]
    z_part = [to_zpeer(10 + q, peer_part.at[q_rows[q]], peer_got.at[q_rows[q]]) for q in range(Q)]
    for c in z_part:
        c.start()
    got = dot(g_pair[0:512, :], a4[...])
    acc[...] = got[0:256] + got[256:512]
    for q in range(Q):
        rows = slice(q * TOK, (q + 1) * TOK)
        acc[rows, :] = acc[rows, :] + xf[:, q * PIECE : (q + 1) * PIECE].astype(F32)

    recv_i()
    lane_i = lax.broadcasted_iota(jnp.int32, (TOK, EXPERTS * 16), 1)
    picks = [jnp.where(lane_i == own_t[0:TOK, 4 + k : 5 + k].astype(jnp.int32), 1.0, 0.0).astype(BF) for k in range(TOP)]
    val = dot(jnp.concatenate(picks, axis=0), iv_got[...])
    inner0 = val[0:64, 0:1] + val[0:64, 64:65]
    inner1 = val[64:128, 0:1] + val[64:128, 64:65]
    rate0, rate1, rate_total = cols_own[:, 4:5], cols_own[:, 5:6], cols_own[:, 6:7]
    weighted = (inner0 * rate0 + inner1 * rate1) / (rate_total * rate_total)
    logit0 = ROUTE_SCALE * (inner0 / rate_total - weighted) * rate0 * (1.0 - rate0)
    logit1 = ROUTE_SCALE * (inner1 / rate_total - weighted) * rate1 * (1.0 - rate1)
    dlogits = jnp.where(lane_e == named[2].astype(jnp.int32), logit0, 0.0)
    dlogits = (dlogits + jnp.where(lane_e == named[3].astype(jnp.int32), logit1, 0.0)).astype(BF)
    rest = dot(dlogits, router[...]) + cg[...].astype(F32)

    def to_next(i, src, dst):
        return pltpu.make_async_remote_copy(
            src_ref=src, dst_ref=dst, send_sem=p_send.at[i], recv_sem=p_recv.at[i], device_id=ahead, device_id_type=MESH
        )

    n_y = [to_next(q, y_send.at[q_rows[q]], y_got.at[q_rows[q]]) for q in range(Q)]
    for q in range(Q):
        rows = slice(q * TOK, (q + 1) * TOK)
        z_part[q].wait_recv()
        y_send[rows, :] = (acc[rows, :] + peer_got[rows, :].astype(F32)).astype(BF)
        n_y[q].start()

    recv5()
    got = dot(g_part[...], a5[...])
    for q in range(S):
        cols = slice(q * PART, (q + 1) * PART)
        dx = rest[:, cols] + got[q * TOK : (q + 1) * TOK] + got[(S + q) * TOK : (S + q + 1) * TOK]
        dx_send[:, cols] = dx.astype(BF)
    n_dx = to_next(4, dx_send, dx_got)
    n_dx.start()

    for q in range(Q):
        n_y[q].wait_recv()
        fwd_out[:, q * PIECE : (q + 1) * PIECE] = y_got[q * TOK : (q + 1) * TOK, :]
    n_dx.wait_recv()
    bwd_out[...] = dx_got[...]

    for sent in (sent4, sent_i, sent5, sent_a):
        sent()
    for copy in z_xg + [z_meta, z_f, z_cols, z_inner, z_kv, n_dx, to_core] + z_back + z_part + n_y + along_x + along_y:
        copy.wait_send()


def handed_on(*refs):
    for i in range(3):
        refs[3 + i][...] = refs[i][...]


def body(x_fwd, routes_fwd, x_bwd, cot_bwd, routes_bwd, router_weight, gate_weight, up_weight, down_weight, attn_input, latent_cot):
    consts = [jnp.asarray(c, BF) for c in permutations()]
    vmem = pl.BlockSpec(memory_space=pltpu.VMEM)
    anywhere = pl.BlockSpec(memory_space=pl.ANY)
    V = pltpu.VMEM
    dma = pltpu.SemaphoreType.DMA
    scratch = [
        V((D, HALF), BF), V((D, HALF), BF), V((HALF, D), BF),
        V((512, PIECE), BF), V((512, PIECE), BF), V((512, PIECE), BF),
        V((8, Q * TOK), F32), V((8, Q * TOK), F32), V((TOK, 128), F32), V((TOK, 128), F32),
        V((WIRE, PIECE), BF), V((WIRE, PIECE), BF),
        V((WIRE, PIECE), BF), V((WIRE, PIECE), BF), V((WIRE, PIECE), BF),
        V((2 * ROWS, D), BF), V((ROWS, D), BF), V((ROWS, HALF), BF), V((ROWS, HALF), BF), V((ROWS, HALF), BF),
        V((2 * ROWS, 128), BF), V((ROWS, 128), BF), V((ROWS, 128), BF),
        V((ROWS, D), BF), V((ROWS, D), BF), V((ROWS, D), BF),
        V((WIRE, PIECE), BF), V((WIRE, PIECE), BF),
        V((WIRE, PART), BF), V((S * 48, PART), BF),
        V((EXPERTS * 16, 128), BF), V((EXPERTS * 16, 128), BF),
        V((2 * S * TOK, WIRE), BF), V((1024, WIRE), BF),
        V((256, PIECE), F32), V((256, PIECE), BF), V((256, PIECE), BF),
        V((EXPERTS * TOK, 128), BF), V((EXPERTS * TOK, 128), BF), V((EXPERTS * TOK, LATENT), BF), V((128, LATENT), F32), V((KV_ROWS, LATENT), F32),
        V((256, PIECE), BF), V((TOK, D), BF), V((256, PIECE), BF), V((TOK, D), BF),
        dma((3,)), dma((18,)), dma((18,)), dma((8, 31)), dma((8, 31)), dma((8,)), dma((7,)), dma((7,)), dma((5,)), dma((5,)),
    ]
    fwd, bwd, kv = pl.pallas_call(
        kernel,
        out_shape=[
            jax.ShapeDtypeStruct((TOK, D), BF),
            jax.ShapeDtypeStruct((TOK, D), BF),
            jax.ShapeDtypeStruct((KV_ROWS, LATENT), F32),
        ],
        in_specs=[vmem] * 12 + [anywhere] * 3,
        out_specs=[vmem] * 3,
        scratch_shapes=scratch,
        compiler_params=pltpu.CompilerParams(collective_id=0, has_side_effects=True, vmem_limit_bytes=63 * 2**20),
        name="layer",
    )(
        x_fwd[0], x_bwd[0], cot_bwd[0], routes_fwd[0].T, routes_bwd[0].T, attn_input[0], latent_cot[0], router_weight[0].T, *consts,
        gate_weight[0, 0], up_weight[0, 0], down_weight[0, 0],
    )
    fwd, bwd, kv = pl.pallas_call(
        handed_on,
        out_shape=[jax.ShapeDtypeStruct(a.shape, a.dtype) for a in (fwd, bwd, kv)],
        in_specs=[vmem] * 3,
        out_specs=[vmem] * 3,
        name="outputs",
    )(fwd, bwd, kv)
    return fwd[None], bwd[None], kv[None]


def solution(mesh):
    tokens = P("pipe", ("dp", "expert"), None)
    in_specs = (
        tokens, tokens, tokens, tokens, tokens,
        P("pipe", None, None),
        P("pipe", "expert", None, "dp"),
        P("pipe", "expert", None, "dp"),
        P("pipe", "expert", "dp", None),
        tokens, tokens,
    )
    return jax.shard_map(body, mesh=mesh, in_specs=in_specs, out_specs=(tokens,) * 3, check_vma=False)
```

```python
import functools

import jax
import jax.numpy as jnp
import numpy as np
from jax import lax
from jax.experimental import pallas as pl
from jax.experimental.pallas import tpu as pltpu
from jax.sharding import PartitionSpec as P

TOP = 2
ROUTE_SCALE = 2.5
CAP = 6
TOK = 64
D = 3584
EXPERTS = 32
HALF = 512
LATENT = 512
Q = 4
PIECE = D // Q
S = 7
PART = D // S
SLOT = 2 * CAP * Q
WIRE = EXPERTS * SLOT
ROWS = EXPERTS * CAP
CHUNK = 8
KV_ROWS = 56
LANES = ((0, 512), (512, PIECE))
MESH = pl.DeviceIdType.MESH
BF = jnp.bfloat16
F32 = jnp.float32

STEPS = [(2, 2), (1, 0), (3, 0), (0, 1), (0, 3), (2, 0), (0, 2), (1, 1), (3, 3), (1, 3), (3, 1), (2, 1), (1, 2), (2, 3), (3, 2)]
STEPS_X = sum(x * 4**i for i, (x, _) in enumerate(STEPS))
STEPS_Y = sum(y * 4**i for i, (_, y) in enumerate(STEPS))


def permutations():
    unpack = np.zeros((CHUNK * SLOT, CHUNK * SLOT), np.float32)
    pack_part = np.zeros((CHUNK * SLOT, S * CHUNK * CAP), np.float32)
    pack_inner = np.zeros((EXPERTS * 16, ROWS), np.float32)
    for s in range(CHUNK):
        for slot in range(CAP):
            for q in range(Q):
                for j in range(2):
                    unpack[j * 192 + q * 48 + s * CAP + slot, s * SLOT + q * 12 + j * CAP + slot] = 1
            for q in range(S):
                pack_part[s * SLOT + q * CAP + slot, q * 48 + s * CAP + slot] = 1
    for s in range(EXPERTS):
        for slot in range(CAP):
            pack_inner[s * 16 + slot, s * CAP + slot] = 1
    return unpack, unpack.T.copy(), pack_part, pack_inner


def dot(a, b):
    return jnp.dot(a, b, preferred_element_type=F32)


def dot_nt(a, b):
    return lax.dot_general(a, b, (((1,), (1,)), ((), ())), preferred_element_type=F32)


def kernel(
    xf, xb, cg, routes_f, routes_b, attn, latent, router, unpack, pack, pack_part, pack_inner,
    gate_hbm, up_hbm, down_hbm,
    fwd_out, bwd_out, kv_out,
    gate, up, down, stack1, stack2, stack3, meta, meta_peer, cols_own, cols_peer,
    w1, w2, a1, a2, a3, x2, x_own, gg, gu, hid, inner, inner_got, inner_sum,
    back_own, back_peer, back_got, fwd_rows, a4, a5, part,
    iv_wire, iv_got, g_part, g_pair, acc, peer_part, peer_got,
    attn_wire, attn_got, latent_got, kv_sum, kv_got, y_send, dx_send, y_got, dx_got,
    load_sem, z_send, z_recv, u_send, u_recv, local_sem, l_send, l_recv, p_send, p_recv,
):
    pi, dp, ex = lax.axis_index("pipe"), lax.axis_index("dp"), lax.axis_index("expert")
    core = lax.rem(ex, 2)
    px = lax.rem(lax.div(ex, 2), 4)
    py = lax.div(ex, 8)
    zpeer = (pi, 1 - dp, ex)
    ahead = (lax.rem(pi + 1, 4), dp, ex)
    behind = (lax.rem(pi + 3, 4), dp, ex)

    loads = [
        pltpu.make_async_copy(src, dst, load_sem.at[i])
        for i, (src, dst) in enumerate([(gate_hbm, gate), (up_hbm, up), (down_hbm, down)])
    ]

    barrier = pltpu.get_barrier_semaphore()
    pl.semaphore_signal(barrier, inc=1, device_id=zpeer, device_id_type=MESH)
    pl.semaphore_signal(barrier, inc=1, device_id=ahead, device_id_type=MESH)
    pl.semaphore_signal(barrier, inc=1, device_id=behind, device_id_type=MESH)

    def greet(o, c):
        pl.semaphore_signal(barrier, inc=1, device_id=(pi, dp, lax.rem(ex + o, EXPERTS)), device_id_type=MESH)
        return c

    lax.fori_loop(1, EXPERTS, greet, 0)
    for load in loads:
        load.start()

    def plane(unit, src, dst, rows, place_at, lanes=None, land=None):
        def piece(e):
            at = pl.ds(pl.multiple_of(e * rows, 16), rows)
            return src.at[at] if lanes is None else src.at[at, lanes]

        landing = pl.ds(pl.multiple_of(place_at * rows, 16), rows)
        landing = dst.at[landing] if land is None else dst.at[landing, land]
        sample = dst.at[pl.ds(0, rows)] if land is None else dst.at[pl.ds(0, rows), land]

        def copy(i, dx, dy, dc):
            to = (lax.rem(py + dy, 4) * 4 + lax.rem(px + dx, 4)) * 2 + lax.rem(core + dc, 2)
            return pltpu.make_async_remote_copy(
                src_ref=piece(to),
                dst_ref=landing,
                send_sem=u_send.at[unit, i],
                recv_sem=u_recv.at[unit, i],
                device_id=(pi, dp, to),
                device_id_type=MESH,
            )

        def local():
            return pltpu.make_async_copy(
                piece(ex),
                landing,
                local_sem.at[unit],
            )

        def start():
            def step(dc, i, c):
                tx, ty = c
                copy(15 * dc + i, lax.rem(tx, 4), lax.rem(ty, 4), dc).start()
                return lax.div(tx, 4), lax.div(ty, 4)

            for dc in range(2):
                lax.fori_loop(0, 15, functools.partial(step, dc), (jnp.int32(STEPS_X), jnp.int32(STEPS_Y)))
            copy(30, 0, 0, 1).start()
            local().start()

        def wait_recv():
            def step(i, c):
                pltpu.make_async_copy(sample, sample, u_recv.at[unit, i]).wait()
                return c

            lax.fori_loop(0, 31, step, 0)
            local().wait()

        def wait_send():
            def step(i, c):
                pltpu.make_async_copy(sample, sample, u_send.at[unit, i]).wait()
                return c

            lax.fori_loop(0, 31, step, 0)

        return start, wait_recv, wait_send

    def to_zpeer(i, src, dst):
        return pltpu.make_async_remote_copy(
            src_ref=src, dst_ref=dst, send_sem=z_send.at[i], recv_sem=z_recv.at[i], device_id=zpeer, device_id_type=MESH
        )

    def place(code_a, code_b, stack, wire, low=0, high=PIECE):
        first = jnp.concatenate([code_a[0:1], code_b[0:1] + float(CAP)], axis=1).astype(jnp.int32)
        second = jnp.concatenate([code_a[1:2], code_b[1:2] + float(CAP)], axis=1).astype(jnp.int32)

        def step(g, c):
            row = lax.broadcasted_iota(jnp.int32, (192, 512), 0) + g * 192
            member = jnp.where((row == first) | (row == second), 1.0, 0.0).astype(BF)
            wire[pl.ds(pl.multiple_of(g * 192, 16), 192), low:high] = dot(member, stack[:, low:high]).astype(BF)
            return c

        lax.fori_loop(0, 8, step, 0)

    def unpacked(wire, *targets):
        def step(c, carry):
            rows = dot(unpack[...], wire[pl.ds(pl.multiple_of(c * 384, 16), 384), :]).astype(BF)
            at = pl.ds(pl.multiple_of(c * 48, 16), 48)
            for j in range(2):
                for q in range(Q):
                    targets[j][at, q * PIECE : (q + 1) * PIECE] = rows[j * 192 + q * 48 : j * 192 + (q + 1) * 48]
            return carry

        lax.fori_loop(0, 4, step, 0)

    x_rows, g_rows = x2.at[pl.ds(0, ROWS)], x2.at[pl.ds(ROWS, ROWS)]

    lane = lax.broadcasted_iota(jnp.int32, (TOK, 128), 1)

    def columns(values):
        out = jnp.zeros((TOK, 128), F32)
        for i, v in enumerate(values):
            out = jnp.where(lane == i, v, out)
        return out

    same_token = lax.broadcasted_iota(jnp.int32, (TOK, Q * TOK), 1) & (TOK - 1)
    same_token = jnp.where(same_token == lax.broadcasted_iota(jnp.int32, (TOK, Q * TOK), 0), 1.0, 0.0).astype(BF)
    named, named_rows = [], []
    for routes in (routes_f, routes_b):
        values = routes[...].astype(F32).astype(BF)
        turned = dot_nt(same_token[:, 0:TOK], values)
        tiled = dot(values, same_token)
        for k in range(TOP):
            named.append(turned[:, k : k + 1])
            named_rows.append(tiled[k : k + 1])
    lane_q = lax.broadcasted_iota(jnp.int32, (TOK, Q * TOK), 1)
    before = lax.broadcasted_iota(jnp.int32, (TOK, Q * TOK), 0) < (lane_q & (TOK - 1))
    offset = ((lane_q[0:1] >> 6) * 12).astype(F32)
    for i in range(4):
        row = named_rows[i]
        same = (named[i // 2 * 2] == row) | (named[i // 2 * 2 + 1] == row)
        slot = jnp.sum(jnp.where(same & before, 1.0, 0.0), axis=0, keepdims=True)
        meta[i : i + 1, :] = row * float(SLOT) + slot + offset
        if i >= 2:
            meta[i + 2 : i + 3, :] = row * 16.0 + slot
            meta[i + 4 : i + 5, :] = row

    for q in range(Q):
        cols = slice(q * PIECE, (q + 1) * PIECE)
        stack1[q * TOK : (q + 1) * TOK, :] = xf[:, cols]
        stack1[256 + q * TOK : 256 + (q + 1) * TOK, :] = xb[:, cols]
        stack3[q * TOK : (q + 1) * TOK, :] = cg[:, cols]
    own = meta[...]
    place(own[0:2], own[2:4], stack1, w1)
    group = (core * 4 + py) * 4
    latent_at = pl.ds(pl.multiple_of((group + px) * TOK, 16), TOK)
    latent_got[latent_at, :] = latent[...]

    pl.semaphore_wait(barrier, 34)
    z_meta = to_zpeer(0, meta, meta_peer)
    top, bottom = pl.ds(0, 256), pl.ds(256, 256)
    z_xg = []
    for i, (low, high) in enumerate(LANES):
        lanes = pl.ds(low, high - low)
        z_xg.append(to_zpeer(14 + 2 * i, stack1.at[bottom, lanes], stack2.at[top, lanes]))
        z_xg.append(to_zpeer(15 + 2 * i, stack3.at[top, lanes], stack2.at[bottom, lanes]))
    z_f = to_zpeer(2, stack1.at[top], stack3.at[bottom])
    z_cols = to_zpeer(3, cols_own, cols_peer)
    z_meta.start()
    z_xg[0].start()
    z_xg[1].start()
    start1, recv1, sent1 = plane(0, w1, a1, SLOT, ex)
    start1()

    def latent_copy(i, at, device):
        return pltpu.make_async_remote_copy(
            src_ref=latent_got.at[at], dst_ref=latent_got.at[at], send_sem=l_send.at[i], recv_sem=l_recv.at[i],
            device_id=(pi, dp, device), device_id_type=MESH,
        )

    along_x = [latent_copy(i, latent_at, (py * 4 + lax.rem(px + 1 + i, 4)) * 2 + core) for i in range(3)]
    row_at = pl.ds(pl.multiple_of(group * TOK, 16), 4 * TOK)
    along_y = [latent_copy(3 + i, row_at, (lax.rem(py + 1 + i, 4) * 4 + px) * 2 + core) for i in range(3)]
    core_at = pl.ds(pl.multiple_of(core * 16 * TOK, 16), 16 * TOK)
    to_core = latent_copy(6, core_at, ex + 1 - 2 * core)
    for c in along_x:
        c.start()

    lane_e = lax.broadcasted_iota(jnp.int32, (TOK, EXPERTS), 1)

    def rates_of(tokens, names):
        logits = dot_nt(tokens[...], router[...])
        return [
            jax.nn.sigmoid(jnp.sum(jnp.where(lane_e == e.astype(jnp.int32), logits, 0.0), axis=1, keepdims=True)) for e in names
        ]

    rate_f = rates_of(xf, named[0:2])
    rate_b = rates_of(xb, named[2:4])
    total_f, total_b = rate_f[0] + rate_f[1], rate_b[0] + rate_b[1]
    gate_f = [ROUTE_SCALE * r / total_f for r in rate_f]
    gate_b = [ROUTE_SCALE * r / total_b for r in rate_b]
    cols_own[...] = columns(gate_f + gate_b + rate_b + [total_b])
    z_cols.start()

    for e in range(EXPERTS):
        halves = []
        for h in range(2):
            first = h * (D // 2) + e * KV_ROWS
            start = min(first // 128 * 128, D - 256)
            window = attn[:, start : start + 256].astype(F32)
            halves.append(pltpu.roll(window, (256 - (first - start) + h * 64) % 256, 1)[:, 0:128])
        attn_wire[e * TOK : (e + 1) * TOK, :] = jnp.where(lane < 64, halves[0], halves[1]).astype(BF)

    z_meta.wait_recv()
    peer = meta_peer[...]
    z_xg[0].wait_recv()
    z_xg[1].wait_recv()
    z_xg[2].start()
    z_xg[3].start()
    second = []
    for unit, (low, high) in zip((1, 7), LANES):
        lanes = pl.ds(low, high - low)
        second.append(plane(unit, w2, a2, SLOT, ex, lanes, lanes))
    place(peer[2:4], peer[2:4], stack2, w2, *LANES[0])
    second[0][0]()
    own_t, peer_t = own.T, peer.T

    def split(values):
        hi = values.astype(BF)
        return hi, (values - hi.astype(F32)).astype(BF)

    lane_w = lax.broadcasted_iota(jnp.int32, (TOK, WIRE), 1)

    def gate_rows(code0, code1, gate0, gate1, offset):
        value = jnp.where(lane_w == code0.astype(jnp.int32) + offset, gate0, 0.0)
        value = value + jnp.where(lane_w == code1.astype(jnp.int32) + offset, gate1, 0.0)
        return split(value)

    def forward_gates(j, m, gates):
        for q in range(Q):
            m_q = m[q * TOK : (q + 1) * TOK]
            hi, lo = gate_rows(m_q[:, 0:1], m_q[:, 1:2], gates[:, 0:1], gates[:, 1:2], j * CAP)
            g_pair[j * 512 + q * TOK : j * 512 + (q + 1) * TOK, :] = hi
            g_pair[j * 512 + 256 + q * TOK : j * 512 + 256 + (q + 1) * TOK, :] = lo

    forward_gates(0, own_t, cols_own[...])
    for q in range(S):
        m = own_t[0:TOK]
        hi, lo = gate_rows(m[:, 2:3], m[:, 3:4], cols_own[:, 2:3], cols_own[:, 3:4], q * CAP)
        g_part[q * TOK : (q + 1) * TOK, :] = hi
        g_part[S * TOK + q * TOK : S * TOK + (q + 1) * TOK, :] = lo
    for c in along_x:
        c.wait_recv()
    for c in along_y:
        c.start()

    z_xg[2].wait_recv()
    z_xg[3].wait_recv()
    z_f.start()
    place(peer[2:4], peer[2:4], stack2, w2, *LANES[1])
    second[1][0]()

    def backward(x, g, rows_out, after=None):
        total = jnp.zeros((ROWS, 1), F32)
        for n in range(HALF // 256):
            cols = slice(n * 256, (n + 1) * 256)
            gate_act = dot(x[...], gate[:, cols])
            up_act = dot(x[...], up[:, cols])
            grad_hidden = dot_nt(g[...], down[cols, :])
            sig = jax.nn.sigmoid(gate_act)
            active = gate_act * sig
            hidden = (active * up_act).astype(BF).astype(F32)
            total = total + jnp.sum(hidden * grad_hidden, axis=1, keepdims=True)
            gg[:, cols] = (grad_hidden * up_act * sig * (1.0 + gate_act * (1.0 - sig))).astype(BF)
            gu[:, cols] = (grad_hidden * active).astype(BF)
        for q in range(Q):
            cols = slice(q * PIECE, (q + 1) * PIECE)
            rows_out[:, cols] = (dot_nt(gg[...], gate[cols, :]) + dot_nt(gu[...], up[cols, :])).astype(BF)
            if after is not None:
                after[q].start()
        return total

    side = lax.broadcasted_iota(jnp.int32, (ROWS, 128), 1) < 64

    def hi_lo(total):
        hi, lo = split(total)
        return jnp.where(side, hi.astype(F32), lo.astype(F32)).astype(BF)

    def forward(j):
        for n in range(HALF // 256):
            cols = slice(n * 256, (n + 1) * 256)
            gate_act = dot(x_rows[...], gate[:, cols])
            up_act = dot(x_rows[...], up[:, cols])
            hid[:, cols] = (gate_act * jax.nn.sigmoid(gate_act) * up_act).astype(BF)
        for q in range(Q):
            rows = dot(hid[...], down[:, q * PIECE : (q + 1) * PIECE]).astype(BF)
            for g in range(4):
                at = g * 384 + j * 192 + q * 48
                fwd_rows[at : at + 48, :] = rows[g * 48 : (g + 1) * 48]

    for load in loads:
        load.wait()
    recv1()
    unpacked(a1, x_rows, x_own)
    forward(0)

    z_f.wait_recv()
    sent1()
    place(own[2:4], peer[0:2], stack3, w1)
    start3, recv3, sent3 = plane(2, w1, a3, SLOT, ex)
    start3()
    for c in along_y:
        c.wait_recv()
    to_core.start()
    z_cols.wait_recv()
    forward_gates(1, peer_t, cols_peer[...])

    q_cols = [pl.ds(q * PIECE, PIECE) for q in range(Q)]
    z_back = [to_zpeer(4 + q, back_peer.at[:, q_cols[q]], back_got.at[:, q_cols[q]]) for q in range(Q)]
    z_inner = to_zpeer(8, inner.at[pl.ds(ROWS, ROWS)], inner_got)
    for unit in second:
        unit[1]()
    unpacked(a2, x_rows, g_rows)
    inner[ROWS : 2 * ROWS, :] = hi_lo(backward(x_rows, g_rows, back_peer, z_back))
    z_inner.start()

    recv3()
    start_a, recv_a, sent_a = plane(5, attn_wire, attn_got, TOK, group + px)
    start_a()
    unpacked(a3, g_rows, x_rows)
    forward(1)
    for unit in second:
        unit[2]()

    def pack_forward(g, c):
        rows = pl.ds(pl.multiple_of(g * 384, 16), 384)
        w2[rows, :] = dot(pack[...], fwd_rows[rows, :]).astype(BF)
        return c

    lax.fori_loop(0, 4, pack_forward, 0)
    start4, recv4, sent4 = plane(3, w2, a4, SLOT, ex)
    start4()

    inner[0:ROWS, :] = hi_lo(backward(x_own, g_rows, back_own))

    to_core.wait_recv()
    recv_a()
    kv_sum[...] = lax.dot_general(attn_got[...], latent_got[...], (((0,), (0,)), ((), ())), preferred_element_type=F32)
    z_kv = to_zpeer(9, kv_sum.at[pl.ds(pl.multiple_of((1 - dp) * 64, 8), KV_ROWS)], kv_got)
    z_kv.start()

    z_inner.wait_recv()
    total = inner[0:ROWS, :].astype(F32) + inner_got[...].astype(F32)
    inner_sum[...] = hi_lo(total[:, 0:1] + total[:, 64:65])
    iv_wire[...] = dot(pack_inner[...], inner_sum[...]).astype(BF)
    start_i, recv_i, sent_i = plane(4, iv_wire, iv_got, 16, ex)
    start_i()
    for c in z_back:
        c.wait_recv()
    sent3()

    def pack_back(g, c):
        rows = pl.ds(pl.multiple_of(g * 48, 16), 48)
        for q in range(S):
            cols = slice(q * PART, (q + 1) * PART)
            part[q * 48 : (q + 1) * 48, :] = (back_own[rows, cols].astype(F32) + back_got[rows, cols].astype(F32)).astype(BF)
        w1[pl.ds(pl.multiple_of(g * 384, 16), 384), 0:PART] = dot(pack_part[...], part[...]).astype(BF)
        return c

    lax.fori_loop(0, 4, pack_back, 0)
    start5, recv5, sent5 = plane(6, w1, a5, SLOT, ex, pl.ds(0, PART))
    start5()
    z_kv.wait_recv()
    kv_out[...] = kv_sum[pl.ds(pl.multiple_of(dp * 64, 8), KV_ROWS), :] + kv_got[...]

    recv4()
    got = dot(g_pair[512:1024, :], a4[...])
    peer_part[...] = (got[0:256] + got[256:512]).astype(BF)
    q_rows = [pl.ds(q * TOK, TOK) for q in range(Q)]
    z_part = [to_zpeer(10 + q, peer_part.at[q_rows[q]], peer_got.at[q_rows[q]]) for q in range(Q)]
    for c in z_part:
        c.start()
    got = dot(g_pair[0:512, :], a4[...])
    acc[...] = got[0:256] + got[256:512]
    for q in range(Q):
        rows = slice(q * TOK, (q + 1) * TOK)
        acc[rows, :] = acc[rows, :] + xf[:, q * PIECE : (q + 1) * PIECE].astype(F32)

    recv_i()
    lane_i = lax.broadcasted_iota(jnp.int32, (TOK, EXPERTS * 16), 1)
    picks = [jnp.where(lane_i == own_t[0:TOK, 4 + k : 5 + k].astype(jnp.int32), 1.0, 0.0).astype(BF) for k in range(TOP)]
    val = dot(jnp.concatenate(picks, axis=0), iv_got[...])
    inner0 = val[0:64, 0:1] + val[0:64, 64:65]
    inner1 = val[64:128, 0:1] + val[64:128, 64:65]
    rate0, rate1, rate_total = cols_own[:, 4:5], cols_own[:, 5:6], cols_own[:, 6:7]
    weighted = (inner0 * rate0 + inner1 * rate1) / (rate_total * rate_total)
    logit0 = ROUTE_SCALE * (inner0 / rate_total - weighted) * rate0 * (1.0 - rate0)
    logit1 = ROUTE_SCALE * (inner1 / rate_total - weighted) * rate1 * (1.0 - rate1)
    dlogits = jnp.where(lane_e == named[2].astype(jnp.int32), logit0, 0.0)
    dlogits = (dlogits + jnp.where(lane_e == named[3].astype(jnp.int32), logit1, 0.0)).astype(BF)
    rest = dot(dlogits, router[...]) + cg[...].astype(F32)

    def to_next(i, src, dst):
        return pltpu.make_async_remote_copy(
            src_ref=src, dst_ref=dst, send_sem=p_send.at[i], recv_sem=p_recv.at[i], device_id=ahead, device_id_type=MESH
        )

    recv5()
    got = dot(g_part[...], a5[...])
    for q in range(S):
        cols = slice(q * PART, (q + 1) * PART)
        dx = rest[:, cols] + got[q * TOK : (q + 1) * TOK] + got[(S + q) * TOK : (S + q + 1) * TOK]
        dx_send[:, cols] = dx.astype(BF)
    n_dx = to_next(4, dx_send, dx_got)
    n_dx.start()

    n_y = [to_next(q, y_send.at[q_rows[q]], y_got.at[q_rows[q]]) for q in range(Q)]
    for q in range(Q):
        rows = slice(q * TOK, (q + 1) * TOK)
        z_part[q].wait_recv()
        y_send[rows, :] = (acc[rows, :] + peer_got[rows, :].astype(F32)).astype(BF)
        n_y[q].start()

    for q in range(Q):
        n_y[q].wait_recv()
        fwd_out[:, q * PIECE : (q + 1) * PIECE] = y_got[q * TOK : (q + 1) * TOK, :]
    n_dx.wait_recv()
    bwd_out[...] = dx_got[...]

    for sent in (sent4, sent_i, sent5, sent_a):
        sent()
    for copy in z_xg + [z_meta, z_f, z_cols, z_inner, z_kv, n_dx, to_core] + z_back + z_part + n_y + along_x + along_y:
        copy.wait_send()


def handed_on(*refs):
    for i in range(3):
        refs[3 + i][...] = refs[i][...]


def body(x_fwd, routes_fwd, x_bwd, cot_bwd, routes_bwd, router_weight, gate_weight, up_weight, down_weight, attn_input, latent_cot):
    consts = [jnp.asarray(c, BF) for c in permutations()]
    vmem = pl.BlockSpec(memory_space=pltpu.VMEM)
    anywhere = pl.BlockSpec(memory_space=pl.ANY)
    V = pltpu.VMEM
    dma = pltpu.SemaphoreType.DMA
    scratch = [
        V((D, HALF), BF), V((D, HALF), BF), V((HALF, D), BF),
        V((512, PIECE), BF), V((512, PIECE), BF), V((512, PIECE), BF),
        V((8, Q * TOK), F32), V((8, Q * TOK), F32), V((TOK, 128), F32), V((TOK, 128), F32),
        V((WIRE, PIECE), BF), V((WIRE, PIECE), BF),
        V((WIRE, PIECE), BF), V((WIRE, PIECE), BF), V((WIRE, PIECE), BF),
        V((2 * ROWS, D), BF), V((ROWS, D), BF), V((ROWS, HALF), BF), V((ROWS, HALF), BF), V((ROWS, HALF), BF),
        V((2 * ROWS, 128), BF), V((ROWS, 128), BF), V((ROWS, 128), BF),
        V((ROWS, D), BF), V((ROWS, D), BF), V((ROWS, D), BF),
        V((WIRE, PIECE), BF), V((WIRE, PIECE), BF),
        V((WIRE, PART), BF), V((S * 48, PART), BF),
        V((EXPERTS * 16, 128), BF), V((EXPERTS * 16, 128), BF),
        V((2 * S * TOK, WIRE), BF), V((1024, WIRE), BF),
        V((256, PIECE), F32), V((256, PIECE), BF), V((256, PIECE), BF),
        V((EXPERTS * TOK, 128), BF), V((EXPERTS * TOK, 128), BF), V((EXPERTS * TOK, LATENT), BF), V((128, LATENT), F32), V((KV_ROWS, LATENT), F32),
        V((256, PIECE), BF), V((TOK, D), BF), V((256, PIECE), BF), V((TOK, D), BF),
        dma((3,)), dma((18,)), dma((18,)), dma((8, 31)), dma((8, 31)), dma((8,)), dma((7,)), dma((7,)), dma((5,)), dma((5,)),
    ]
    fwd, bwd, kv = pl.pallas_call(
        kernel,
        out_shape=[
            jax.ShapeDtypeStruct((TOK, D), BF),
            jax.ShapeDtypeStruct((TOK, D), BF),
            jax.ShapeDtypeStruct((KV_ROWS, LATENT), F32),
        ],
        in_specs=[vmem] * 12 + [anywhere] * 3,
        out_specs=[vmem] * 3,
        scratch_shapes=scratch,
        compiler_params=pltpu.CompilerParams(collective_id=0, has_side_effects=True, vmem_limit_bytes=63 * 2**20),
        name="layer",
    )(
        x_fwd[0], x_bwd[0], cot_bwd[0], routes_fwd[0].T, routes_bwd[0].T, attn_input[0], latent_cot[0], router_weight[0].T, *consts,
        gate_weight[0, 0], up_weight[0, 0], down_weight[0, 0],
    )
    fwd, bwd, kv = pl.pallas_call(
        handed_on,
        out_shape=[jax.ShapeDtypeStruct(a.shape, a.dtype) for a in (fwd, bwd, kv)],
        in_specs=[vmem] * 3,
        out_specs=[vmem] * 3,
        name="outputs",
    )(fwd, bwd, kv)
    return fwd[None], bwd[None], kv[None]


def solution(mesh):
    tokens = P("pipe", ("dp", "expert"), None)
    in_specs = (
        tokens, tokens, tokens, tokens, tokens,
        P("pipe", None, None),
        P("pipe", "expert", None, "dp"),
        P("pipe", "expert", None, "dp"),
        P("pipe", "expert", "dp", None),
        tokens, tokens,
    )
    return jax.shard_map(body, mesh=mesh, in_specs=in_specs, out_specs=(tokens,) * 3, check_vma=False)
```
